256 devices in a mesh: rep: 32 (over z_lo, y, core), fsdp: 8 (over z_hi, x).
Axes of the slice: x: 4, y: 4, z: 8 (z_hi: 2, z_lo: 4; z = z_hi * 4 + z_lo), core: 2. Of those that a mesh axis runs over, the one named last changes fastest.
Arguments:
- params: bfloat16 [32, 7168, 2048], P('rep', 'fsdp'), may hold values from -6 to 6
- hidden_acts: bfloat16 [32, 1024, 7168], P('rep', 'fsdp'), may hold values from -6 to 6
- out_grads: bfloat16 [32, 1024, 2048], P('rep', 'fsdp'), may hold values from -6 to 6
- step_counts: int32 [32], P('rep'), may hold values from 1 to 32
- outer_z: float32 [7168, 2048], P('fsdp', 'rep'), may hold values from -4 to 4
- outer_x: float32 [7168, 2048], P('fsdp', 'rep'), may hold values from -4 to 4
Outputs:
- new_z: float32 [7168, 2048], P('fsdp', 'rep')
- new_x: float32 [7168, 2048], P('fsdp', 'rep')
- new_y: bfloat16 [7168, 2048], P('fsdp')
The draws below stay inside these ranges and needn't reach their ends.
All inputs are finite; a program needn't handle non-finite values.
Results may differ from the reference program's by a relative error of at most 0.0055.
Values may be sent and summed in bfloat16 or wider, within the bound.
A program may use at most 128 MiB of HBM per device.

```python
import jax
import jax.numpy as jnp
from jax import lax

D = 2048
FFW = 7168
ROUND = 3
REPS = 32
TOK_REP = 1024


def with_ends(entries, stream_key, smallest, high):
    index_at = [jax.random.randint(jax.random.fold_in(stream_key, axis), (), 0, length) for axis, length in enumerate(entries.shape)]
    widest = entries.shape.index(max(entries.shape))
    neighbour = index_at[:widest] + [(index_at[widest] + 1) % entries.shape[widest]] + index_at[widest + 1:]
    return entries.at[tuple(index_at)].set(smallest).at[tuple(neighbour)].set(high)


def raised(result, rng, source, target, parts, factor):
    def block_of(dim):
        return (jnp.arange(result.shape[dim]) // (result.shape[dim] // parts)).reshape((-1,) + (1,) * (result.ndim - 1 - dim))

    first = jax.random.permutation(rng, parts)[block_of(target)]
    far = (block_of(target) + parts // 2) % parts
    return jnp.where((block_of(source) == first) | (block_of(source) == far), factor * result, result)


def block_levels(own_key, shape, split, smallest, top_value):
    level = 1.0
    for axis_at, blocks in split:
        draws = jax.random.uniform(jax.random.fold_in(jax.random.fold_in(own_key, 6), axis_at), (blocks,), jnp.float32, smallest / len(split), top_value / len(split))
        level = level * jnp.repeat(jnp.exp(draws), shape[axis_at] // blocks).reshape((-1,) + (1,) * (len(shape) - 1 - axis_at))
    return level


def scatter_about(rng, extent, scale, limit, pieces=(), held_as=jnp.bfloat16):
    level = block_levels(rng, extent, pieces, -0.22, 0.18) if pieces else 1.0
    values = jax.random.normal(rng, extent, jnp.float32) * scale * level
    return jnp.minimum(jnp.maximum(values, -limit), limit).astype(held_as)


def bell_draw_with(key, shape, scale, most, shards, heavy, kind=jnp.bfloat16):
    drawn = scale * jax.random.normal(key, shape, jnp.float32)
    if shards:
        drawn = drawn * block_levels(key, shape, shards, -0.22, 0.18)
    return jnp.clip(raised(drawn, jax.random.fold_in(key, 3), *heavy), -most, most).astype(kind)


def setup_inputs(seed: int = 0) -> dict:
    key_of = jax.random.split(jax.random.key(seed), 7)
    return {
        "params": bell_draw_with(key_of[0], (REPS, FFW, D), 1.0, 6.0, ((0, 32), (1, 8)), (0, 2, 32, 2.75)),
        "hidden_acts": scatter_about(key_of[1], (REPS, TOK_REP, FFW), 1.0, 6.0, ((0, 32), (1, 8))),
        "out_grads": scatter_about(key_of[2], (REPS, TOK_REP, D), 1.0, 6.0, ((0, 32), (1, 8))),
        "step_counts": with_ends(jax.random.randint(key_of[3], (REPS,), 1, 33), jax.random.fold_in(key_of[3], 1), 1, 32).astype(jnp.int32),
        "outer_z": scatter_about(key_of[4], (FFW, D), 0.5, 4.0, ((0, 8), (1, 32)), jnp.float32),
        "outer_x": scatter_about(key_of[5], (FFW, D), 0.5, 4.0, ((0, 8), (1, 32)), jnp.float32),
    }


def reference(params, hidden_acts, out_grads, step_counts, outer_z, outer_x):
    def one_replica(summed, index):
        grad = jnp.dot(hidden_acts[index].T, out_grads[index], preferred_element_type=jnp.float32)
        inner = (params[index].astype(jnp.float32) - 0.1 * grad).astype(jnp.bfloat16)
        weight = step_counts[index].astype(jnp.float32)
        return summed + weight * inner.astype(jnp.float32), None

    start = jnp.zeros(outer_z.shape, jnp.float32)
    summed, unused = lax.scan(one_replica, start, jnp.arange(REPS, dtype=jnp.int32))
    total = jnp.sum(step_counts).astype(jnp.float32)
    anchor = 0.1 * outer_z + 0.9 * outer_x
    pseudo = anchor - summed / total
    new_z = outer_z - 0.7 * pseudo
    mixing = 1.0 / (ROUND + 1.0)
    new_x = (1.0 - mixing) * outer_x + mixing * new_z
    new_y = (0.1 * new_z + 0.9 * new_x).astype(jnp.bfloat16)
    return new_z, new_x, new_y
```

```python
import functools

import jax
import jax.numpy as jnp
from jax import lax
from jax.experimental import pallas as pl
from jax.experimental.pallas import tpu as pltpu
from jax.sharding import Mesh
from jax.sharding import PartitionSpec as P

ROUND = 3
MESH = pl.DeviceIdType.MESH
CHUNKS = (128, 128, 128, 128, 128, 128, 128)
F32 = jnp.float32
BF16 = jnp.bfloat16


def kernel(
    p_ref, h_ref, g_ref, n_ref, z_ref, x_ref,
    zo_ref, xo_ref, yo_ref,
    hb, at, ab, gb, pb, wp, cb, r1a, r1b, r2a, r2b, zs, yg, yr, zt, xt, zf, xf, nzt, nxt, wt, ty, tz,
    in_sem, b_send, b_recv, sib_send, sib_recv, a_send, a_recv,
    y1_send, y1_recv, y2_send, y2_recv, z_send, z_recv, g1_send, g1_recv, g2_send, g2_recv,
    o_loc, o_send, o_recv, t_send, t_recv, e_send, e_recv,
):
    x, y, c = lax.axis_index("x"), lax.axis_index("y"), lax.axis_index("c")
    zh, zl = lax.axis_index("zh"), lax.axis_index("zl")
    z = zh * 4 + zl
    owner = zh == c
    other = 1 - c

    def plus(v, d, n=4):
        return lax.rem(v + d, n)

    def rdma(src, dst, ss, rs, **where):
        return pltpu.make_async_remote_copy(
            src_ref=src, dst_ref=dst, send_sem=ss, recv_sem=rs, device_id=where, device_id_type=MESH
        )

    def await_bytes(ref, sem):
        pltpu.make_async_copy(ref, ref, sem).wait()

    starts = [sum(CHUNKS[:m]) for m in range(len(CHUNKS))]
    rows_of = [slice(s, s + r) for s, r in zip(starts, CHUNKS)]
    n_chunks = len(CHUNKS)

    g_in = pltpu.make_async_copy(g_ref, gb.at[0, pl.ds(0, 128)], in_sem.at[0])
    g_in.start()
    h_in = pltpu.make_async_copy(h_ref, hb, in_sem.at[1])
    h_in.start()
    mine = pl.ds(pl.multiple_of(c * 64, 64), 64)
    theirs = pl.ds(pl.multiple_of(other * 64, 64), 64)
    z_in = pltpu.make_async_copy(z_ref, zt.at[mine], in_sem.at[2])
    z_in.start()
    x_in = pltpu.make_async_copy(x_ref, xt.at[mine], in_sem.at[3])
    x_in.start()
    p_in = pltpu.make_async_copy(p_ref, pb.at[0], in_sem.at[4])

    @pl.when(owner)
    def _():
        p_in.start()

    wt[0] = jnp.full((8, 128), n_ref[0].astype(F32), F32)

    barrier = pltpu.get_barrier_semaphore()
    peers = [{"c": other}]
    peers += [{"x": plus(x, d), "c": k} for d in (1, 2, 3) for k in (c, other)]
    peers += [{"y": plus(y, d)} for d in (1, 2, 3)]
    peers += [{"zh": plus(z, d, 8) // 4, "zl": plus(z, d, 4)} for d in range(1, 8)]
    for peer in peers:
        pl.semaphore_signal(barrier, inc=1, device_id=peer, device_id_type=MESH)
    pl.semaphore_wait(barrier, len(peers))

    xp, xm = plus(x, 1), plus(x, 3)
    g_in.wait()
    lo, hi = pl.ds(0, 64), pl.ds(64, 64)
    own_lo, own_hi = gb.at[0, pl.ds(0, 64)], gb.at[0, pl.ds(64, 64)]
    from_left = [gb.at[0, pl.ds(128, 64)], gb.at[0, pl.ds(192, 64)]]
    from_right = [gb.at[0, pl.ds(384, 64)], gb.at[0, pl.ds(448, 64)]]
    far = [gb.at[0, pl.ds(256, 64)], gb.at[0, pl.ds(320, 64)]]
    b_copies = [
        rdma(own_lo, from_left[0], b_send.at[0], b_recv.at[0], x=xp),
        rdma(own_hi, from_right[1], b_send.at[3], b_recv.at[3], x=xm),
        rdma(own_hi, from_left[1], b_send.at[1], b_recv.at[1], x=xp),
        rdma(own_lo, from_right[0], b_send.at[2], b_recv.at[2], x=xm),
    ]
    for copy in b_copies:
        copy.start()

    def to_sibling(k):
        part = pl.ds(k * 128, 128)
        return rdma(gb.at[0, part], gb.at[1, part], sib_send.at[k], sib_recv.at[k], c=other)

    w_copy = rdma(wt.at[0], wt.at[1], e_send.at[0], e_recv.at[0], c=other)
    w_copy.start()
    sib_copies = [to_sibling(k) for k in range(4)]
    sib_copies[0].start()
    p_copy = rdma(p_ref, pb.at[1], e_send.at[1], e_recv.at[1], c=other)

    @pl.when(jnp.logical_not(owner))
    def _():
        p_copy.start()

    z_copy = rdma(z_ref, zt.at[mine], e_send.at[2], e_recv.at[2], c=other)
    z_copy.start()
    x_copy = rdma(x_ref, xt.at[mine], e_send.at[3], e_recv.at[3], c=other)
    x_copy.start()

    h_in.wait()

    @pl.loop(0, 8)
    def _(q):
        for i in range(7):
            cols = pl.ds(pl.multiple_of(q * 896 + i * 128, 128), 128)
            at[q, i * 128 : (i + 1) * 128, :] = hb[:, cols].T

    w_copy.wait()
    ty[0] = wt[0] + wt[1]
    ty_copies = [rdma(ty.at[0], ty.at[d], t_send.at[d - 1], t_recv.at[d - 1], y=plus(y, d)) for d in (1, 2, 3)]
    for copy in ty_copies:
        copy.start()

    def send_inputs(m):
        r = rows_of[m]
        for dx in (2, 1, 3, 0):
            for dc in (0, 1):
                core = plus(c, dc, 2)
                to_x = plus(x, dx)
                src = at.at[core * 4 + to_x, r]
                dst = ab.at[r, pl.ds((dc * 4 + dx) * 128, 128)]
                if dx == 0 and dc == 0:
                    pltpu.make_async_copy(src, dst, a_recv.at[m]).start()
                else:
                    rdma(src, dst, a_send.at[m], a_recv.at[m], x=to_x, c=core).start()

    b_copies[0].wait_recv()
    fwd_a = rdma(from_left[0], far[0], b_send.at[4], b_recv.at[4], x=xp)
    fwd_a.start()
    b_copies[1].wait_recv()
    fwd_b = rdma(from_right[1], far[1], b_send.at[5], b_recv.at[5], x=xm)
    fwd_b.start()
    send_inputs(0)
    if n_chunks > 1:
        send_inputs(1)

    for copy in ty_copies:
        copy.wait()
    tz[0] = ty[0] + ty[1] + ty[2] + ty[3]
    tz_copies = [rdma(tz.at[0], tz.at[d], t_send.at[d + 2], t_recv.at[d + 2], zl=plus(zl, d)) for d in (1, 2, 3)]
    for copy in tz_copies:
        copy.start()

    w_own, w_sib = wt[0][0:1, :], wt[1][0:1, :]

    @pl.when(owner)
    def _():
        p_in.wait()
        p_copy.wait_recv()

        @pl.loop(0, 56)
        def _(i):
            r = pl.ds(pl.multiple_of(i * 16, 16), 16)
            for j in range(16):
                k = slice(j * 128, (j + 1) * 128)
                wp[r, k] = w_own * pb[0, r, k].astype(F32) + w_sib * pb[1, r, k].astype(F32)

    @pl.when(jnp.logical_not(owner))
    def _():
        p_copy.wait_send()

        @pl.loop(0, 56)
        def _(i):
            r = pl.ds(pl.multiple_of(i * 16, 16), 16)
            wp[r, :] = jnp.zeros((16, 2048), F32)

    z_in.wait()
    x_in.wait()
    z_copy.wait()
    x_copy.wait()
    for i in range(7):
        k = slice(i * 128, (i + 1) * 128)
        zf[k, :] = zt[:, k].T
        xf[k, :] = xt[:, k].T
    for copy in tz_copies:
        copy.wait()
    total = (tz[0] + tz[1] + tz[2] + tz[3])[0:1, :]

    b_copies[2].wait_recv()
    sib_copies[1].start()
    b_copies[3].wait_recv()
    sib_copies[3].start()
    fwd_a.wait_recv()
    fwd_b.wait_recv()
    sib_copies[2].start()
    for copy in sib_copies:
        copy.wait_recv()

    yp, ym, yf = plus(y, 1), plus(y, 3), plus(y, 2)

    def y_first(m):
        r = rows_of[m]
        return [
            rdma(cb.at[yf, pl.ds(0, 2), r], r1a.at[:, r], y1_send.at[m, 0], y1_recv.at[m, 0], y=yp),
            rdma(cb.at[yf, pl.ds(2, 2), r], r1b.at[:, r], y1_send.at[m, 1], y1_recv.at[m, 1], y=ym),
        ]

    def y_second(m):
        r = rows_of[m]
        return [
            rdma(cb.at[yp, :, r], r2a.at[:, r], y2_send.at[m, 0], y2_recv.at[m, 0], y=yp),
            rdma(cb.at[ym, :, r], r2b.at[:, r], y2_send.at[m, 1], y2_recv.at[m, 1], y=ym),
        ]

    def multiply(m):
        r = rows_of[m]
        await_bytes(ab.at[r], a_recv.at[m])
        if m + 2 < n_chunks:
            send_inputs(m + 2)

        @pl.loop(0, 4)
        def _(q):
            cols = pl.ds(pl.multiple_of(q * 512, 512), 512)
            d_own = jnp.dot(ab[r, 0:512], gb[0, :, cols], preferred_element_type=F32)
            d_sib = jnp.dot(ab[r, 512:1024], gb[1, :, cols], preferred_element_type=F32)
            for j in range(4):
                k = slice(j * 128, (j + 1) * 128)
                base = wp[r, pl.ds(pl.multiple_of(q * 512 + j * 128, 128), 128)]
                cb[j, q, r] = (base - 0.1 * (w_own * d_own[:, k] + w_sib * d_sib[:, k])).astype(BF16)

        for copy in y_first(m):
            copy.start()

    def merge(m):
        r = rows_of[m]
        first, second = y_first(m), y_second(m)
        first[0].wait_recv()
        for j in (0, 1):
            cb[yp, j, r] = (cb[yp, j, r].astype(F32) + r1a[j, r].astype(F32)).astype(BF16)
        second[0].start()
        first[1].wait_recv()
        for j in (2, 3):
            cb[ym, j, r] = (cb[ym, j, r].astype(F32) + r1b[j - 2, r].astype(F32)).astype(BF16)
        second[1].start()

    def z_copies(m):
        r = rows_of[m]
        return [
            rdma(cb.at[y, plus(zl, d), r], zs.at[z, r], z_send.at[m], z_recv.at[m], zh=c, zl=plus(zl, d))
            for d in range(4)
        ]

    def along_z(m):
        r = rows_of[m]
        for copy in y_second(m):
            copy.wait_recv()
        for j in range(4):
            cb[y, j, r] = (cb[y, j, r].astype(F32) + r2a[j, r].astype(F32) + r2b[j, r].astype(F32)).astype(BF16)
        copies = z_copies(m)
        for d in (2, 1, 3):
            copies[d].start()

        @pl.when(owner)
        def _():
            pltpu.make_async_copy(cb.at[y, zl, r], zs.at[z, r], z_recv.at[m]).start()

        @pl.when(jnp.logical_not(owner))
        def _():
            copies[0].start()

    def finish(m):
        r = rows_of[m]
        await_bytes(zs.at[:, r], z_recv.at[m])
        summed = zs[0, r].astype(F32)
        for k in range(1, 8):
            summed = summed + zs[k, r].astype(F32)
        outer_z, outer_x = zf[r, :], xf[r, :]
        anchor = 0.1 * outer_z + 0.9 * outer_x
        pseudo = anchor - summed / total
        new_z = outer_z - 0.7 * pseudo
        mixing = 1.0 / (ROUND + 1.0)
        new_x = (1.0 - mixing) * outer_x + mixing * new_z
        yg[y, zl, r] = (0.1 * new_z + 0.9 * new_x).astype(BF16)
        for d in (1, 2, 3):
            rdma(yg.at[y, zl, r], yg.at[y, zl, r], g1_send.at[m], g1_recv.at[m], zl=plus(zl, d)).start()
        nzt[:, r] = new_z.T
        nxt[:, r] = new_x.T

    def gather_y(m):
        r = rows_of[m]
        await_bytes(yg.at[y, pl.ds(0, 3), r], g1_recv.at[m])
        for d in (2, 1, 3):
            rdma(yg.at[y, :, r], yg.at[y, :, r], g2_send.at[m], g2_recv.at[m], y=plus(y, d)).start()

    def out_copies(m):
        r = rows_of[m]
        return (
            pltpu.make_async_copy(yr.at[r], yo_ref.at[r], o_loc.at[m]),
            rdma(yr.at[r], yo_ref.at[r], o_send.at[m], o_recv.at[m], c=other),
        )

    def deliver(m):
        r = rows_of[m]
        await_bytes(yg.at[pl.ds(0, 3), :, r], g2_recv.at[m])
        for j in range(16):
            yr[r, j * 128 : (j + 1) * 128] = yg[j % 4, j // 4, r]
        for copy in out_copies(m):
            copy.start()

    state_out = (
        pltpu.make_async_copy(nzt.at[mine], zo_ref, in_sem.at[5]),
        pltpu.make_async_copy(nxt.at[mine], xo_ref, in_sem.at[6]),
    )
    state_away = (
        rdma(nzt.at[theirs], zo_ref, e_send.at[4], e_recv.at[4], c=other),
        rdma(nxt.at[theirs], xo_ref, e_send.at[5], e_recv.at[5], c=other),
    )

    for t in range(n_chunks + 5):
        if t < n_chunks:
            multiply(t)
        if 0 <= t - 1 < n_chunks:
            merge(t - 1)
        if 0 <= t - 2 < n_chunks:
            along_z(t - 2)

        @pl.when(owner)
        def _():
            if 0 <= t - 3 < n_chunks:
                finish(t - 3)
            if t - 3 == n_chunks - 1:
                for copy in (*state_out, *state_away):
                    copy.start()
            if 0 <= t - 4 < n_chunks:
                gather_y(t - 4)
            if 0 <= t - 5 < n_chunks:
                deliver(t - 5)

    for copy in (*b_copies, fwd_a, fwd_b, *sib_copies):
        copy.wait_send()
    for m in range(n_chunks):
        r = rows_of[m]
        await_bytes(ab.at[r, pl.ds(0, 896)], a_send.at[m])
        for copy in (*y_first(m), *y_second(m)):
            copy.wait_send()

    @pl.when(owner)
    def _():
        for m in range(n_chunks):
            r = rows_of[m]
            await_bytes(zs.at[pl.ds(0, 3), r], z_send.at[m])
            await_bytes(yg.at[0, pl.ds(0, 3), r], g1_send.at[m])
            await_bytes(yg.at[pl.ds(0, 3), :, r], g2_send.at[m])
            here, away = out_copies(m)
            here.wait()
            away.wait_send()
        for copy in state_out:
            copy.wait()
        for copy in state_away:
            copy.wait_send()

    @pl.when(jnp.logical_not(owner))
    def _():
        for m in range(n_chunks):
            await_bytes(zs.at[pl.ds(0, 4), rows_of[m]], z_send.at[m])
            out_copies(m)[1].wait_recv()
        for copy in state_away:
            copy.wait_recv()


def local(params, hidden_acts, out_grads, step_counts, outer_z, outer_x):
    n = len(CHUNKS)
    dma = pltpu.SemaphoreType.DMA
    hbm = pl.BlockSpec(memory_space=pl.ANY)
    new_z, new_x, new_y = pl.pallas_call(
        kernel,
        name="outer_sync",
        out_shape=(
            jax.ShapeDtypeStruct((64, 896), F32),
            jax.ShapeDtypeStruct((64, 896), F32),
            jax.ShapeDtypeStruct((896, 2048), BF16),
        ),
        in_specs=[hbm, hbm, hbm, pl.BlockSpec(memory_space=pltpu.SMEM), hbm, hbm],
        out_specs=(hbm, hbm, hbm),
        scratch_shapes=[
            pltpu.VMEM((128, 7168), BF16),
            pltpu.VMEM((8, 896, 128), BF16),
            pltpu.VMEM((896, 1024), BF16),
            pltpu.VMEM((2, 512, 2048), BF16),
            pltpu.VMEM((2, 896, 2048), BF16),
            pltpu.VMEM((896, 2048), F32),
            pltpu.VMEM((4, 4, 896, 128), BF16),
            pltpu.VMEM((2, 896, 128), BF16),
            pltpu.VMEM((2, 896, 128), BF16),
            pltpu.VMEM((4, 896, 128), BF16),
            pltpu.VMEM((4, 896, 128), BF16),
            pltpu.VMEM((8, 896, 128), BF16),
            pltpu.VMEM((4, 4, 896, 128), BF16),
            pltpu.VMEM((896, 2048), BF16),
            pltpu.VMEM((128, 896), F32),
            pltpu.VMEM((128, 896), F32),
            pltpu.VMEM((896, 128), F32),
            pltpu.VMEM((896, 128), F32),
            pltpu.VMEM((128, 896), F32),
            pltpu.VMEM((128, 896), F32),
            pltpu.VMEM((2, 8, 128), F32),
            pltpu.VMEM((4, 8, 128), F32),
            pltpu.VMEM((4, 8, 128), F32),
            dma((7,)),
            dma((6,)), dma((6,)),
            dma((4,)), dma((4,)),
            dma((n,)), dma((n,)),
            dma((n, 2)), dma((n, 2)),
            dma((n, 2)), dma((n, 2)),
            dma((n,)), dma((n,)),
            dma((n,)), dma((n,)),
            dma((n,)), dma((n,)),
            dma((n,)), dma((n,)), dma((n,)),
            dma((6,)), dma((6,)),
            dma((6,)), dma((6,)),
        ],
        compiler_params=pltpu.CompilerParams(
            collective_id=0, has_side_effects=True, vmem_limit_bytes=60 * 2**20
        ),
        cost_estimate=pl.CostEstimate(flops=3_760_000_000, bytes_accessed=12_000_000, transcendentals=0),
    )(params[0], hidden_acts[0], out_grads[0], step_counts, outer_z.T, outer_x.T)
    return new_z.T, new_x.T, new_y


def solution(mesh):
    split = Mesh(mesh.devices.reshape(4, 4, 2, 2, 4), ("zl", "y", "c", "zh", "x"))
    rep, fsdp = ("zl", "y", "c"), ("zh", "x")
    placed = (
        P(rep, fsdp, None),
        P(rep, fsdp, None),
        P(rep, fsdp, None),
        P(rep),
        P(fsdp, rep),
        P(fsdp, rep),
    )
    return jax.shard_map(
        local,
        mesh=split,
        in_specs=placed,
        out_specs=(P(fsdp, rep), P(fsdp, rep), P(fsdp, None)),
        check_vma=False,
    )
```

```python
import functools

import jax
import jax.numpy as jnp
from jax import lax
from jax.experimental import pallas as pl
from jax.experimental.pallas import tpu as pltpu
from jax.sharding import Mesh
from jax.sharding import PartitionSpec as P

ROUND = 3
MESH = pl.DeviceIdType.MESH
CHUNKS = (128, 128, 128, 128, 128, 128, 64, 64)
SKEW = (1, 2, 3, 4, 5, 6)
RELAY = (0, 1, 2, 3, 4, 5)
Y_FIRST = ()
F32 = jnp.float32
BF16 = jnp.bfloat16


def kernel(
    p_ref, h_ref, g_ref, n_ref, z_ref, x_ref,
    zo_ref, xo_ref, yo_ref,
    hb, at, ab, gb, pb, wp, cb, r1a, r1b, r2a, r2b, zs, yg, zt, xt, zf, xf, nzt, nxt, wt, ty, tz,
    in_sem, b_send, b_recv, sib_send, sib_recv, a_send, a_recv,
    y1_send, y1_recv, y2_send, y2_recv, z_send, z_recv, g1_send, g1_recv, g2_send, g2_recv,
    o_send, o_recv, t_send, t_recv, e_send, e_recv,
):
    x, y, c = lax.axis_index("x"), lax.axis_index("y"), lax.axis_index("c")
    zh, zl = lax.axis_index("zh"), lax.axis_index("zl")
    z = zh * 4 + zl
    owner = zh == c
    other = 1 - c

    def plus(v, d, n=4):
        return lax.rem(v + d, n)

    def rdma(src, dst, ss, rs, **where):
        return pltpu.make_async_remote_copy(
            src_ref=src, dst_ref=dst, send_sem=ss, recv_sem=rs, device_id=where, device_id_type=MESH
        )

    def await_bytes(ref, sem):
        pltpu.make_async_copy(ref, ref, sem).wait()

    starts = [sum(CHUNKS[:m]) for m in range(len(CHUNKS))]
    rows_of = [slice(s, s + r) for s, r in zip(starts, CHUNKS)]
    n_chunks = len(CHUNKS)

    g_in = pltpu.make_async_copy(g_ref, gb.at[0, pl.ds(0, 128)], in_sem.at[0])
    g_in.start()
    h_in = pltpu.make_async_copy(h_ref, hb, in_sem.at[1])
    h_in.start()
    mine = pl.ds(pl.multiple_of(c * 64, 64), 64)
    theirs = pl.ds(pl.multiple_of(other * 64, 64), 64)
    z_in = pltpu.make_async_copy(z_ref, zt.at[mine], in_sem.at[2])
    z_in.start()
    x_in = pltpu.make_async_copy(x_ref, xt.at[mine], in_sem.at[3])
    x_in.start()
    p_in = pltpu.make_async_copy(p_ref, pb.at[0], in_sem.at[4])

    @pl.when(owner)
    def _():
        p_in.start()

    wt[0] = jnp.full((8, 128), n_ref[0].astype(F32), F32)

    barrier = pltpu.get_barrier_semaphore()
    peers = [{"c": other}]
    peers += [{"x": plus(x, d), "c": k} for d in (1, 2, 3) for k in (c, other)]
    peers += [{"y": plus(y, d)} for d in (1, 2, 3)]
    peers += [{"zh": plus(z, d, 8) // 4, "zl": plus(z, d, 4)} for d in range(1, 8)]
    for peer in peers:
        pl.semaphore_signal(barrier, inc=1, device_id=peer, device_id_type=MESH)
    pl.semaphore_wait(barrier, len(peers))

    xp, xm = plus(x, 1), plus(x, 3)
    g_in.wait()
    lo, hi = pl.ds(0, 64), pl.ds(64, 64)
    own_lo, own_hi = gb.at[0, pl.ds(0, 64)], gb.at[0, pl.ds(64, 64)]
    from_left = [gb.at[0, pl.ds(128, 64)], gb.at[0, pl.ds(192, 64)]]
    from_right = [gb.at[0, pl.ds(384, 64)], gb.at[0, pl.ds(448, 64)]]
    far = [gb.at[0, pl.ds(256, 64)], gb.at[0, pl.ds(320, 64)]]
    b_copies = [
        rdma(own_lo, from_left[0], b_send.at[0], b_recv.at[0], x=xp),
        rdma(own_hi, from_right[1], b_send.at[3], b_recv.at[3], x=xm),
        rdma(own_hi, from_left[1], b_send.at[1], b_recv.at[1], x=xp),
        rdma(own_lo, from_right[0], b_send.at[2], b_recv.at[2], x=xm),
    ]
    for copy in b_copies[:2]:
        copy.start()

    def to_sibling(k):
        part = pl.ds(k * 128, 128)
        return rdma(gb.at[0, part], gb.at[1, part], sib_send.at[k], sib_recv.at[k], c=other)

    w_copy = rdma(wt.at[0], wt.at[1], e_send.at[0], e_recv.at[0], c=other)
    w_copy.start()
    sib_copies = [to_sibling(k) for k in range(4)]
    sib_copies[0].start()
    p_copy = rdma(p_ref, pb.at[1], e_send.at[1], e_recv.at[1], c=other)

    @pl.when(jnp.logical_not(owner))
    def _():
        p_copy.start()

    z_copy = rdma(z_ref, zt.at[mine], e_send.at[2], e_recv.at[2], c=other)
    z_copy.start()
    x_copy = rdma(x_ref, xt.at[mine], e_send.at[3], e_recv.at[3], c=other)
    x_copy.start()

    h_in.wait()

    def transpose(q):
        for i in range(7):
            cols = pl.ds(pl.multiple_of(q * 896 + i * 128, 128), 128)
            at[q, i * 128 : (i + 1) * 128, :] = hb[:, cols].T

    pl.loop(0, 3)(transpose)
    for copy in b_copies[2:]:
        copy.start()
    pl.loop(3, 8)(transpose)

    w_copy.wait()
    ty[0] = wt[0] + wt[1]
    ty_copies = [rdma(ty.at[0], ty.at[d], t_send.at[d - 1], t_recv.at[d - 1], y=plus(y, d)) for d in (1, 2, 3)]
    for copy in ty_copies:
        copy.start()

    def send_inputs(m):
        r = rows_of[m]
        for dx in (2, 1, 3, 0):
            for dc in (0, 1):
                core = plus(c, dc, 2)
                to_x = plus(x, dx)
                src = at.at[core * 4 + to_x, r]
                dst = ab.at[r, pl.ds((dc * 4 + dx) * 128, 128)]
                if dx == 0 and dc == 0:
                    pltpu.make_async_copy(src, dst, a_recv.at[m]).start()
                else:
                    rdma(src, dst, a_send.at[m], a_recv.at[m], x=to_x, c=core).start()

    b_copies[0].wait_recv()
    fwd_a = rdma(from_left[0], far[0], b_send.at[4], b_recv.at[4], x=xp)
    fwd_a.start()
    b_copies[1].wait_recv()
    fwd_b = rdma(from_right[1], far[1], b_send.at[5], b_recv.at[5], x=xm)
    fwd_b.start()
    send_inputs(0)
    if n_chunks > 1:
        send_inputs(1)

    for copy in ty_copies:
        copy.wait()
    tz[0] = ty[0] + ty[1] + ty[2] + ty[3]
    tz_copies = [rdma(tz.at[0], tz.at[d], t_send.at[d + 2], t_recv.at[d + 2], zl=plus(zl, d)) for d in (1, 2, 3)]
    for copy in tz_copies:
        copy.start()

    w_own, w_sib = wt[0][0:1, :], wt[1][0:1, :]

    @pl.when(owner)
    def _():
        p_in.wait()
        p_copy.wait_recv()

        @pl.loop(0, 56)
        def _(i):
            r = pl.ds(pl.multiple_of(i * 16, 16), 16)
            for j in range(16):
                k = slice(j * 128, (j + 1) * 128)
                wp[r, k] = w_own * pb[0, r, k].astype(F32) + w_sib * pb[1, r, k].astype(F32)

    @pl.when(jnp.logical_not(owner))
    def _():
        p_copy.wait_send()

        @pl.loop(0, 56)
        def _(i):
            r = pl.ds(pl.multiple_of(i * 16, 16), 16)
            wp[r, :] = jnp.zeros((16, 2048), F32)

    z_in.wait()
    x_in.wait()
    z_copy.wait()
    x_copy.wait()
    for i in range(7):
        k = slice(i * 128, (i + 1) * 128)
        zf[k, :] = zt[:, k].T
        xf[k, :] = xt[:, k].T
    for copy in tz_copies:
        copy.wait()
    total = (tz[0] + tz[1] + tz[2] + tz[3])[0:1, :]

    b_copies[2].wait_recv()
    sib_copies[1].start()
    b_copies[3].wait_recv()
    sib_copies[3].start()
    fwd_a.wait_recv()
    fwd_b.wait_recv()
    sib_copies[2].start()
    for copy in sib_copies:
        copy.wait_recv()

    yp, ym, yf = plus(y, 1), plus(y, 3), plus(y, 2)

    def y_first(m):
        r = rows_of[m]
        return [
            rdma(cb.at[yf, pl.ds(0, 2), r], r1a.at[:, r], y1_send.at[m, 0], y1_recv.at[m, 0], y=yp),
            rdma(cb.at[yf, pl.ds(2, 2), r], r1b.at[:, r], y1_send.at[m, 1], y1_recv.at[m, 1], y=ym),
        ]

    def y_second(m):
        r = rows_of[m]
        return [
            rdma(cb.at[yp, :, r], r2a.at[:, r], y2_send.at[m, 0], y2_recv.at[m, 0], y=yp),
            rdma(cb.at[ym, :, r], r2b.at[:, r], y2_send.at[m, 1], y2_recv.at[m, 1], y=ym),
        ]

    def multiply(m):
        r = rows_of[m]
        await_bytes(ab.at[r], a_recv.at[m])
        if m + 2 < n_chunks:
            send_inputs(m + 2)

        @pl.loop(0, 4)
        def _(q):
            cols = pl.ds(pl.multiple_of(q * 512, 512), 512)
            d_own = jnp.dot(ab[r, 0:512], gb[0, :, cols], preferred_element_type=F32)
            d_sib = jnp.dot(ab[r, 512:1024], gb[1, :, cols], preferred_element_type=F32)
            for j in range(4):
                k = slice(j * 128, (j + 1) * 128)
                base = wp[r, pl.ds(pl.multiple_of(q * 512 + j * 128, 128), 128)]
                cb[j, q, r] = (base - 0.1 * (w_own * d_own[:, k] + w_sib * d_sib[:, k])).astype(BF16)

        for copy in y_first(m):
            copy.start()

    def merge(m):
        r = rows_of[m]
        first, second = y_first(m), y_second(m)
        first[0].wait_recv()
        for j in (0, 1):
            cb[yp, j, r] = (cb[yp, j, r].astype(F32) + r1a[j, r].astype(F32)).astype(BF16)
        second[0].start()
        first[1].wait_recv()
        for j in (2, 3):
            cb[ym, j, r] = (cb[ym, j, r].astype(F32) + r1b[j - 2, r].astype(F32)).astype(BF16)
        second[1].start()

    def z_copies(m):
        r = rows_of[m]
        return [
            rdma(cb.at[y, plus(zl, d), r], zs.at[z, r], z_send.at[m], z_recv.at[m], zh=c, zl=plus(zl, d))
            for d in range(4)
        ]

    def along_z(m):
        r = rows_of[m]
        for copy in y_second(m):
            copy.wait_recv()
        for j in range(4):
            cb[y, j, r] = (cb[y, j, r].astype(F32) + r2a[j, r].astype(F32) + r2b[j, r].astype(F32)).astype(BF16)
        copies = z_copies(m)
        for d in (2, 1, 3):
            copies[d].start()

        @pl.when(owner)
        def _():
            pltpu.make_async_copy(cb.at[y, zl, r], zs.at[z, r], z_recv.at[m]).start()

        @pl.when(jnp.logical_not(owner))
        def _():
            copies[0].start()

    def finish(m):
        r = rows_of[m]
        await_bytes(zs.at[:, r], z_recv.at[m])
        summed = zs[0, r].astype(F32)
        for k in range(1, 8):
            summed = summed + zs[k, r].astype(F32)
        outer_z, outer_x = zf[r, :], xf[r, :]
        anchor = 0.1 * outer_z + 0.9 * outer_x
        pseudo = anchor - summed / total
        new_z = outer_z - 0.7 * pseudo
        mixing = 1.0 / (ROUND + 1.0)
        new_x = (1.0 - mixing) * outer_x + mixing * new_z
        yg[y, zl, r] = (0.1 * new_z + 0.9 * new_x).astype(BF16)
        for d in (2, 1, 3):
            where = {"y": plus(y, d)} if m in Y_FIRST else {"zl": plus(zl, d)}
            rdma(yg.at[y, zl, r], yg.at[y, zl, r], g1_send.at[m], g1_recv.at[m], **where).start()
        zf[r, :] = new_z
        xf[r, :] = new_x

    def gather_y(m):
        r = rows_of[m]
        await_bytes(yg.at[y, pl.ds(0, 3), r], g1_recv.at[m])
        if m in Y_FIRST:
            part, steps = yg.at[:, zl, r], [({"zl": plus(zl, d)}, 0) for d in (2, 1, 3)]
        elif m in RELAY:
            part, steps = yg.at[y, :, r], [({"y": yp}, 0), ({"y": ym}, 1)]
        else:
            part, steps = yg.at[y, :, r], [({"y": plus(y, d)}, 0) for d in (2, 1, 3)]
        for where, k in steps:
            rdma(part, part, g2_send.at[m], g2_recv.at[m, k], **where).start()

    def pass_y(m):
        r = rows_of[m]
        await_bytes(yg.at[ym, :, r], g2_recv.at[m, 0])
        part = yg.at[ym, pl.ds(0, 2), r]
        rdma(part, part, g2_send.at[m], g2_recv.at[m, 2], y=yp).start()
        await_bytes(yg.at[yp, :, r], g2_recv.at[m, 1])
        part = yg.at[yp, pl.ds(2, 2), r]
        rdma(part, part, g2_send.at[m], g2_recv.at[m, 3], y=ym).start()

    def out_away(m):
        r = rows_of[m]
        return rdma(yo_ref.at[r], yo_ref.at[r], o_send.at[m], o_recv.at[m], c=other)

    def deliver(m):
        r = rows_of[m]
        if m in RELAY:
            await_bytes(yg.at[yf, pl.ds(0, 2), r], g2_recv.at[m, 2])
            await_bytes(yg.at[yf, pl.ds(2, 2), r], g2_recv.at[m, 3])
        else:
            await_bytes(yg.at[pl.ds(0, 3), :, r], g2_recv.at[m, 0])
        for j in range(16):
            yo_ref[r, j * 128 : (j + 1) * 128] = yg[j % 4, j // 4, r]
        out_away(m).start()

    state_out = (
        pltpu.make_async_copy(nzt.at[mine], zo_ref, in_sem.at[5]),
        pltpu.make_async_copy(nxt.at[mine], xo_ref, in_sem.at[6]),
    )
    state_away = (
        rdma(nzt.at[theirs], zo_ref, e_send.at[4], e_recv.at[4], c=other),
        rdma(nxt.at[theirs], xo_ref, e_send.at[5], e_recv.at[5], c=other),
    )

    s_merge, s_along, s_finish, s_gather, s_pass, s_deliver = SKEW
    chunks = range(n_chunks)
    for t in range(n_chunks + s_deliver):
        if t in chunks:
            multiply(t)
        if t - s_merge in chunks:
            merge(t - s_merge)
        if t - s_along in chunks:
            along_z(t - s_along)

        @pl.when(owner)
        def _():
            if t - s_finish in chunks:
                finish(t - s_finish)
            if t - s_gather in chunks:
                gather_y(t - s_gather)
            if t - s_finish == n_chunks - 1:
                for i in range(7):
                    k = slice(i * 128, (i + 1) * 128)
                    nzt[:, k] = zf[k, :].T
                    nxt[:, k] = xf[k, :].T
                for copy in (*state_out, *state_away):
                    copy.start()
            if t - s_pass in chunks and t - s_pass in RELAY:
                pass_y(t - s_pass)
            if t - s_deliver in chunks:
                deliver(t - s_deliver)

    for copy in (*b_copies, fwd_a, fwd_b, *sib_copies):
        copy.wait_send()
    for m in range(n_chunks):
        r = rows_of[m]
        await_bytes(ab.at[r, pl.ds(0, 896)], a_send.at[m])
        for copy in (*y_first(m), *y_second(m)):
            copy.wait_send()

    @pl.when(owner)
    def _():
        for m in range(n_chunks):
            r = rows_of[m]
            await_bytes(zs.at[pl.ds(0, 3), r], z_send.at[m])
            await_bytes(yg.at[0, pl.ds(0, 3), r], g1_send.at[m])
            await_bytes(yg.at[pl.ds(0, 3), :, r], g2_send.at[m])
            out_away(m).wait_send()
        for copy in state_out:
            copy.wait()
        for copy in state_away:
            copy.wait_send()

    @pl.when(jnp.logical_not(owner))
    def _():
        for m in range(n_chunks):
            await_bytes(zs.at[pl.ds(0, 4), rows_of[m]], z_send.at[m])
            out_away(m).wait_recv()
        for copy in state_away:
            copy.wait_recv()


def local(params, hidden_acts, out_grads, step_counts, outer_z, outer_x):
    n = len(CHUNKS)
    dma = pltpu.SemaphoreType.DMA
    hbm = pl.BlockSpec(memory_space=pl.ANY)
    vmem = pl.BlockSpec(memory_space=pltpu.VMEM)
    new_z, new_x, new_y = pl.pallas_call(
        kernel,
        name="outer_sync",
        out_shape=(pltpu.VMEM((64, 896), F32), pltpu.VMEM((64, 896), F32), pltpu.VMEM((896, 2048), BF16)),
        in_specs=[hbm, hbm, hbm, pl.BlockSpec(memory_space=pltpu.SMEM), hbm, hbm],
        out_specs=(vmem, vmem, vmem),
        scratch_shapes=[
            pltpu.VMEM((128, 7168), BF16),
            pltpu.VMEM((8, 896, 128), BF16),
            pltpu.VMEM((896, 1024), BF16),
            pltpu.VMEM((2, 512, 2048), BF16),
            pltpu.VMEM((2, 896, 2048), BF16),
            pltpu.VMEM((896, 2048), F32),
            pltpu.VMEM((4, 4, 896, 128), BF16),
            pltpu.VMEM((2, 896, 128), BF16),
            pltpu.VMEM((2, 896, 128), BF16),
            pltpu.VMEM((4, 896, 128), BF16),
            pltpu.VMEM((4, 896, 128), BF16),
            pltpu.VMEM((8, 896, 128), BF16),
            pltpu.VMEM((4, 4, 896, 128), BF16),
            pltpu.VMEM((128, 896), F32),
            pltpu.VMEM((128, 896), F32),
            pltpu.VMEM((896, 128), F32),
            pltpu.VMEM((896, 128), F32),
            pltpu.VMEM((128, 896), F32),
            pltpu.VMEM((128, 896), F32),
            pltpu.VMEM((2, 8, 128), F32),
            pltpu.VMEM((4, 8, 128), F32),
            pltpu.VMEM((4, 8, 128), F32),
            dma((7,)),
            dma((6,)), dma((6,)),
            dma((4,)), dma((4,)),
            dma((n,)), dma((n,)),
            dma((n, 2)), dma((n, 2)),
            dma((n, 2)), dma((n, 2)),
            dma((n,)), dma((n,)),
            dma((n,)), dma((n,)),
            dma((n,)), dma((n, 4)),
            dma((n,)), dma((n,)),
            dma((6,)), dma((6,)),
            dma((6,)), dma((6,)),
        ],
        compiler_params=pltpu.CompilerParams(
            collective_id=0, has_side_effects=True, vmem_limit_bytes=50 * 2**20
        ),
        cost_estimate=pl.CostEstimate(flops=3_760_000_000, bytes_accessed=12_000_000, transcendentals=0),
    )(params[0], hidden_acts[0], out_grads[0], step_counts, outer_z.T, outer_x.T)
    return new_z.T, new_x.T, new_y


def solution(mesh):
    split = Mesh(mesh.devices.reshape(4, 4, 2, 2, 4), ("zl", "y", "c", "zh", "x"))
    rep, fsdp = ("zl", "y", "c"), ("zh", "x")
    placed = (
        P(rep, fsdp, None),
        P(rep, fsdp, None),
        P(rep, fsdp, None),
        P(rep),
        P(fsdp, rep),
        P(fsdp, rep),
    )
    return jax.shard_map(
        local,
        mesh=split,
        in_specs=placed,
        out_specs=(P(fsdp, rep), P(fsdp, rep), P(fsdp, None)),
        check_vma=False,
    )
```

```python
import functools

import jax
import jax.numpy as jnp
from jax import lax
from jax.experimental import pallas as pl
from jax.experimental.pallas import tpu as pltpu
from jax.sharding import Mesh
from jax.sharding import PartitionSpec as P

ROUND = 3
MESH = pl.DeviceIdType.MESH
CHUNKS = (128, 128, 128, 128, 128, 128, 64, 64)
READY = {"multiply": 0, "merge": 1.01, "along_z": 2.02, "finish": 3.03, "gather_y": 4.04, "pass_y": 5.05, "deliver": 6.06}
AHEAD = 2
RELAY = (0, 1, 2, 3, 4, 5)
Y_FIRST = ()
F32 = jnp.float32
BF16 = jnp.bfloat16


def kernel(
    p_ref, h_ref, g_ref, n_ref, z_ref, x_ref,
    zo_ref, xo_ref, yo_ref,
    hb, at, ab, gb, pb, wp, cb, r1a, r1b, r2a, r2b, zs, yg, zt, xt, zf, xf, nzt, nxt, wt, ty, tz,
    in_sem, b_send, b_recv, sib_send, sib_recv, a_send, a_recv,
    y1_send, y1_recv, y2_send, y2_recv, z_send, z_recv, g1_send, g1_recv, g2_send, g2_recv,
    o_send, o_recv, t_send, t_recv, e_send, e_recv,
):
    x, y, c = lax.axis_index("x"), lax.axis_index("y"), lax.axis_index("c")
    zh, zl = lax.axis_index("zh"), lax.axis_index("zl")
    z = zh * 4 + zl
    owner = zh == c
    other = 1 - c

    def plus(v, d, n=4):
        return lax.rem(v + d, n)

    def rdma(src, dst, ss, rs, **where):
        return pltpu.make_async_remote_copy(
            src_ref=src, dst_ref=dst, send_sem=ss, recv_sem=rs, device_id=where, device_id_type=MESH
        )

    def await_bytes(ref, sem):
        pltpu.make_async_copy(ref, ref, sem).wait()

    starts = [sum(CHUNKS[:m]) for m in range(len(CHUNKS))]
    rows_of = [slice(s, s + r) for s, r in zip(starts, CHUNKS)]
    n_chunks = len(CHUNKS)

    g_in = pltpu.make_async_copy(g_ref, gb.at[0, pl.ds(0, 128)], in_sem.at[0])
    g_in.start()
    h_in = pltpu.make_async_copy(h_ref, hb, in_sem.at[1])
    h_in.start()
    mine = pl.ds(pl.multiple_of(c * 64, 64), 64)
    theirs = pl.ds(pl.multiple_of(other * 64, 64), 64)
    z_in = pltpu.make_async_copy(z_ref, zt.at[mine], in_sem.at[2])
    z_in.start()
    x_in = pltpu.make_async_copy(x_ref, xt.at[mine], in_sem.at[3])
    x_in.start()
    p_in = pltpu.make_async_copy(p_ref, pb.at[0], in_sem.at[4])

    @pl.when(owner)
    def _():
        p_in.start()

    wt[0] = jnp.full((8, 128), n_ref[0].astype(F32), F32)

    barrier = pltpu.get_barrier_semaphore()
    peers = [{"zh": plus(z, d, 8) // 4, "zl": plus(z, d, 4)} for d in (4, 3, 5, 2, 6, 1, 7)]
    peers += [{"x": plus(x, d), "c": k} for d in (1, 2, 3) for k in (c, other)]
    peers += [{"y": plus(y, d)} for d in (1, 2, 3)]
    peers += [{"c": other}]
    for peer in peers:
        pl.semaphore_signal(barrier, inc=1, device_id=peer, device_id_type=MESH)
    pl.semaphore_wait(barrier, len(peers))

    xp, xm = plus(x, 1), plus(x, 3)
    g_in.wait()
    lo, hi = pl.ds(0, 64), pl.ds(64, 64)
    own_lo, own_hi = gb.at[0, pl.ds(0, 64)], gb.at[0, pl.ds(64, 64)]
    from_left = [gb.at[0, pl.ds(128, 64)], gb.at[0, pl.ds(192, 64)]]
    from_right = [gb.at[0, pl.ds(384, 64)], gb.at[0, pl.ds(448, 64)]]
    far = [gb.at[0, pl.ds(256, 64)], gb.at[0, pl.ds(320, 64)]]
    b_copies = [
        rdma(own_lo, from_left[0], b_send.at[0], b_recv.at[0], x=xp),
        rdma(own_hi, from_right[1], b_send.at[3], b_recv.at[3], x=xm),
        rdma(own_hi, from_left[1], b_send.at[1], b_recv.at[1], x=xp),
        rdma(own_lo, from_right[0], b_send.at[2], b_recv.at[2], x=xm),
    ]
    for copy in b_copies[:2]:
        copy.start()

    def to_sibling(k):
        part = pl.ds(k * 128, 128)
        return rdma(gb.at[0, part], gb.at[1, part], sib_send.at[k], sib_recv.at[k], c=other)

    w_copy = rdma(wt.at[0], wt.at[1], e_send.at[0], e_recv.at[0], c=other)
    w_copy.start()
    sib_copies = [to_sibling(k) for k in range(4)]
    sib_copies[0].start()
    p_copy = rdma(p_ref, pb.at[1], e_send.at[1], e_recv.at[1], c=other)

    @pl.when(jnp.logical_not(owner))
    def _():
        p_copy.start()

    z_copy = rdma(z_ref, zt.at[mine], e_send.at[2], e_recv.at[2], c=other)
    z_copy.start()
    x_copy = rdma(x_ref, xt.at[mine], e_send.at[3], e_recv.at[3], c=other)
    x_copy.start()

    h_in.wait()

    def transpose(q):
        for i in range(7):
            cols = pl.ds(pl.multiple_of(q * 896 + i * 128, 128), 128)
            at[q, i * 128 : (i + 1) * 128, :] = hb[:, cols].T

    pl.loop(0, 3)(transpose)
    for copy in b_copies[2:]:
        copy.start()
    pl.loop(3, 8)(transpose)

    w_copy.wait()
    ty[0] = wt[0] + wt[1]
    ty_copies = [rdma(ty.at[0], ty.at[d], t_send.at[d - 1], t_recv.at[d - 1], y=plus(y, d)) for d in (1, 2, 3)]
    for copy in ty_copies:
        copy.start()

    def send_inputs(m):
        r = rows_of[m]
        for dx in (2, 1, 3, 0):
            for dc in (0, 1):
                core = plus(c, dc, 2)
                to_x = plus(x, dx)
                src = at.at[core * 4 + to_x, r]
                dst = ab.at[r, pl.ds((dc * 4 + dx) * 128, 128)]
                if dx == 0 and dc == 0:
                    pltpu.make_async_copy(src, dst, a_recv.at[m]).start()
                else:
                    rdma(src, dst, a_send.at[m], a_recv.at[m], x=to_x, c=core).start()

    b_copies[0].wait_recv()
    fwd_a = rdma(from_left[0], far[0], b_send.at[4], b_recv.at[4], x=xp)
    fwd_a.start()
    b_copies[1].wait_recv()
    fwd_b = rdma(from_right[1], far[1], b_send.at[5], b_recv.at[5], x=xm)
    fwd_b.start()

    for copy in ty_copies:
        copy.wait()
    tz[0] = ty[0] + ty[1] + ty[2] + ty[3]
    tz_copies = [rdma(tz.at[0], tz.at[d], t_send.at[d + 2], t_recv.at[d + 2], zl=plus(zl, d)) for d in (1, 2, 3)]
    for copy in tz_copies:
        copy.start()

    w_own, w_sib = wt[0][0:1, :], wt[1][0:1, :]

    @pl.when(owner)
    def _():
        p_in.wait()
        p_copy.wait_recv()

        @pl.loop(0, 56)
        def _(i):
            r = pl.ds(pl.multiple_of(i * 16, 16), 16)
            for j in range(16):
                k = slice(j * 128, (j + 1) * 128)
                wp[r, k] = w_own * pb[0, r, k].astype(F32) + w_sib * pb[1, r, k].astype(F32)

    @pl.when(jnp.logical_not(owner))
    def _():
        p_copy.wait_send()

        @pl.loop(0, 56)
        def _(i):
            r = pl.ds(pl.multiple_of(i * 16, 16), 16)
            wp[r, :] = jnp.zeros((16, 2048), F32)

    z_in.wait()
    x_in.wait()
    z_copy.wait()
    x_copy.wait()
    for i in range(7):
        k = slice(i * 128, (i + 1) * 128)
        zf[k, :] = zt[:, k].T
        xf[k, :] = xt[:, k].T
    for copy in tz_copies:
        copy.wait()
    total = (tz[0] + tz[1] + tz[2] + tz[3])[0:1, :]

    b_copies[2].wait_recv()
    sib_copies[1].start()
    b_copies[3].wait_recv()
    sib_copies[3].start()
    send_inputs(0)
    fwd_a.wait_recv()
    fwd_b.wait_recv()
    sib_copies[2].start()
    for m in range(1, AHEAD):
        send_inputs(m)
    for copy in sib_copies:
        copy.wait_recv()

    yp, ym, yf = plus(y, 1), plus(y, 3), plus(y, 2)

    def y_first(m):
        r = rows_of[m]
        return [
            rdma(cb.at[yf, pl.ds(0, 2), r], r1a.at[:, r], y1_send.at[m, 0], y1_recv.at[m, 0], y=yp),
            rdma(cb.at[yf, pl.ds(2, 2), r], r1b.at[:, r], y1_send.at[m, 1], y1_recv.at[m, 1], y=ym),
        ]

    def y_second(m):
        r = rows_of[m]
        return [
            rdma(cb.at[yp, :, r], r2a.at[:, r], y2_send.at[m, 0], y2_recv.at[m, 0], y=yp),
            rdma(cb.at[ym, :, r], r2b.at[:, r], y2_send.at[m, 1], y2_recv.at[m, 1], y=ym),
        ]

    def multiply(m):
        r = rows_of[m]
        await_bytes(ab.at[r], a_recv.at[m])
        if m + AHEAD < n_chunks:
            send_inputs(m + AHEAD)

        @pl.loop(0, 4)
        def _(q):
            cols = pl.ds(pl.multiple_of(q * 512, 512), 512)
            d_own = jnp.dot(ab[r, 0:512], gb[0, :, cols], preferred_element_type=F32)
            d_sib = jnp.dot(ab[r, 512:1024], gb[1, :, cols], preferred_element_type=F32)
            for j in range(4):
                k = slice(j * 128, (j + 1) * 128)
                base = wp[r, pl.ds(pl.multiple_of(q * 512 + j * 128, 128), 128)]
                cb[j, q, r] = (base - 0.1 * (w_own * d_own[:, k] + w_sib * d_sib[:, k])).astype(BF16)

        for copy in y_first(m):
            copy.start()

    def merge(m):
        r = rows_of[m]
        first, second = y_first(m), y_second(m)
        first[0].wait_recv()
        for j in (0, 1):
            cb[yp, j, r] = (cb[yp, j, r].astype(F32) + r1a[j, r].astype(F32)).astype(BF16)
        second[0].start()
        first[1].wait_recv()
        for j in (2, 3):
            cb[ym, j, r] = (cb[ym, j, r].astype(F32) + r1b[j - 2, r].astype(F32)).astype(BF16)
        second[1].start()

    def z_copies(m):
        r = rows_of[m]
        return [
            rdma(cb.at[y, plus(zl, d), r], zs.at[z, r], z_send.at[m], z_recv.at[m], zh=c, zl=plus(zl, d))
            for d in range(4)
        ]

    def along_z(m):
        r = rows_of[m]
        for copy in y_second(m):
            copy.wait_recv()
        for j in range(4):
            cb[y, j, r] = (cb[y, j, r].astype(F32) + r2a[j, r].astype(F32) + r2b[j, r].astype(F32)).astype(BF16)
        copies = z_copies(m)
        for d in (2, 1, 3):
            copies[d].start()

        @pl.when(owner)
        def _():
            pltpu.make_async_copy(cb.at[y, zl, r], zs.at[z, r], z_recv.at[m]).start()

        @pl.when(jnp.logical_not(owner))
        def _():
            copies[0].start()

    def finish(m):
        r = rows_of[m]
        await_bytes(zs.at[:, r], z_recv.at[m])
        summed = zs[0, r].astype(F32)
        for k in range(1, 8):
            summed = summed + zs[k, r].astype(F32)
        outer_z, outer_x = zf[r, :], xf[r, :]
        anchor = 0.1 * outer_z + 0.9 * outer_x
        pseudo = anchor - summed / total
        new_z = outer_z - 0.7 * pseudo
        mixing = 1.0 / (ROUND + 1.0)
        new_x = (1.0 - mixing) * outer_x + mixing * new_z
        yg[y, zl, r] = (0.1 * new_z + 0.9 * new_x).astype(BF16)
        for d in (2, 1, 3):
            where = {"y": plus(y, d)} if m in Y_FIRST else {"zl": plus(zl, d)}
            rdma(yg.at[y, zl, r], yg.at[y, zl, r], g1_send.at[m], g1_recv.at[m], **where).start()
        zf[r, :] = new_z
        xf[r, :] = new_x

    def gather_y(m):
        r = rows_of[m]
        await_bytes(yg.at[y, pl.ds(0, 3), r], g1_recv.at[m])
        if m in Y_FIRST:
            part, steps = yg.at[:, zl, r], [({"zl": plus(zl, d)}, 0) for d in (2, 1, 3)]
        elif m in RELAY:
            part, steps = yg.at[y, :, r], [({"y": yp}, 0), ({"y": ym}, 1)]
        else:
            part, steps = yg.at[y, :, r], [({"y": plus(y, d)}, 0) for d in (2, 1, 3)]
        for where, k in steps:
            rdma(part, part, g2_send.at[m], g2_recv.at[m, k], **where).start()

    def pass_y(m):
        r = rows_of[m]
        await_bytes(yg.at[ym, :, r], g2_recv.at[m, 0])
        part = yg.at[ym, pl.ds(0, 2), r]
        rdma(part, part, g2_send.at[m], g2_recv.at[m, 2], y=yp).start()
        await_bytes(yg.at[yp, :, r], g2_recv.at[m, 1])
        part = yg.at[yp, pl.ds(2, 2), r]
        rdma(part, part, g2_send.at[m], g2_recv.at[m, 3], y=ym).start()

    def out_away(m):
        r = rows_of[m]
        return rdma(yo_ref.at[r], yo_ref.at[r], o_send.at[m], o_recv.at[m], c=other)

    def deliver(m):
        r = rows_of[m]
        if m in RELAY:
            await_bytes(yg.at[yf, pl.ds(0, 2), r], g2_recv.at[m, 2])
            await_bytes(yg.at[yf, pl.ds(2, 2), r], g2_recv.at[m, 3])
        else:
            await_bytes(yg.at[pl.ds(0, 3), :, r], g2_recv.at[m, 0])
        for j in range(16):
            yo_ref[r, j * 128 : (j + 1) * 128] = yg[j % 4, j // 4, r]
        out_away(m).start()

    state_out = (
        pltpu.make_async_copy(nzt.at[mine], zo_ref, in_sem.at[5]),
        pltpu.make_async_copy(nxt.at[mine], xo_ref, in_sem.at[6]),
    )
    state_away = (
        rdma(nzt.at[theirs], zo_ref, e_send.at[4], e_recv.at[4], c=other),
        rdma(nxt.at[theirs], xo_ref, e_send.at[5], e_recv.at[5], c=other),
    )

    def state(m):
        for i in range(7):
            k = slice(i * 128, (i + 1) * 128)
            nzt[:, k] = zf[k, :].T
            nxt[:, k] = xf[k, :].T
        for copy in (*state_out, *state_away):
            copy.start()

    stages = {
        "multiply": multiply, "merge": merge, "along_z": along_z,
        "finish": finish, "gather_y": gather_y, "pass_y": pass_y, "deliver": deliver,
    }
    order = sorted(
        (starts[m] / 128 + ready, k, m)
        for m in range(n_chunks)
        for k, (stage, ready) in enumerate(READY.items())
        if stage != "pass_y" or m in RELAY
    )
    names = list(READY)
    for _, k, m in order:
        if k < 3:
            stages[names[k]](m)
        else:

            @pl.when(owner)
            def _():
                stages[names[k]](m)
                if names[k] == "finish" and m == n_chunks - 1:
                    state(m)

    for copy in (*b_copies, fwd_a, fwd_b, *sib_copies):
        copy.wait_send()
    for m in range(n_chunks):
        r = rows_of[m]
        await_bytes(ab.at[r, pl.ds(0, 896)], a_send.at[m])
        for copy in (*y_first(m), *y_second(m)):
            copy.wait_send()

    @pl.when(owner)
    def _():
        for m in range(n_chunks):
            r = rows_of[m]
            await_bytes(zs.at[pl.ds(0, 3), r], z_send.at[m])
            await_bytes(yg.at[0, pl.ds(0, 3), r], g1_send.at[m])
            await_bytes(yg.at[pl.ds(0, 3), :, r], g2_send.at[m])
            out_away(m).wait_send()
        for copy in state_out:
            copy.wait()
        for copy in state_away:
            copy.wait_send()

    @pl.when(jnp.logical_not(owner))
    def _():
        for m in range(n_chunks):
            await_bytes(zs.at[pl.ds(0, 4), rows_of[m]], z_send.at[m])
            out_away(m).wait_recv()
        for copy in state_away:
            copy.wait_recv()


def local(params, hidden_acts, out_grads, step_counts, outer_z, outer_x):
    n = len(CHUNKS)
    dma = pltpu.SemaphoreType.DMA
    hbm = pl.BlockSpec(memory_space=pl.ANY)
    vmem = pl.BlockSpec(memory_space=pltpu.VMEM)
    new_z, new_x, new_y = pl.pallas_call(
        kernel,
        name="outer_sync",
        out_shape=(pltpu.VMEM((64, 896), F32), pltpu.VMEM((64, 896), F32), pltpu.VMEM((896, 2048), BF16)),
        in_specs=[hbm, hbm, hbm, pl.BlockSpec(memory_space=pltpu.SMEM), hbm, hbm],
        out_specs=(vmem, vmem, vmem),
        scratch_shapes=[
            pltpu.VMEM((128, 7168), BF16),
            pltpu.VMEM((8, 896, 128), BF16),
            pltpu.VMEM((896, 1024), BF16),
            pltpu.VMEM((2, 512, 2048), BF16),
            pltpu.VMEM((2, 896, 2048), BF16),
            pltpu.VMEM((896, 2048), F32),
            pltpu.VMEM((4, 4, 896, 128), BF16),
            pltpu.VMEM((2, 896, 128), BF16),
            pltpu.VMEM((2, 896, 128), BF16),
            pltpu.VMEM((4, 896, 128), BF16),
            pltpu.VMEM((4, 896, 128), BF16),
            pltpu.VMEM((8, 896, 128), BF16),
            pltpu.VMEM((4, 4, 896, 128), BF16),
            pltpu.VMEM((128, 896), F32),
            pltpu.VMEM((128, 896), F32),
            pltpu.VMEM((896, 128), F32),
            pltpu.VMEM((896, 128), F32),
            pltpu.VMEM((128, 896), F32),
            pltpu.VMEM((128, 896), F32),
            pltpu.VMEM((2, 8, 128), F32),
            pltpu.VMEM((4, 8, 128), F32),
            pltpu.VMEM((4, 8, 128), F32),
            dma((7,)),
            dma((6,)), dma((6,)),
            dma((4,)), dma((4,)),
            dma((n,)), dma((n,)),
            dma((n, 2)), dma((n, 2)),
            dma((n, 2)), dma((n, 2)),
            dma((n,)), dma((n,)),
            dma((n,)), dma((n,)),
            dma((n,)), dma((n, 4)),
            dma((n,)), dma((n,)),
            dma((6,)), dma((6,)),
            dma((6,)), dma((6,)),
        ],
        compiler_params=pltpu.CompilerParams(
            collective_id=0, has_side_effects=True, vmem_limit_bytes=50 * 2**20
        ),
        cost_estimate=pl.CostEstimate(flops=3_760_000_000, bytes_accessed=12_000_000, transcendentals=0),
    )(params[0], hidden_acts[0], out_grads[0], step_counts, outer_z.T, outer_x.T)
    return new_z.T, new_x.T, new_y


def solution(mesh):
    split = Mesh(mesh.devices.reshape(4, 4, 2, 2, 4), ("zl", "y", "c", "zh", "x"))
    rep, fsdp = ("zl", "y", "c"), ("zh", "x")
    placed = (
        P(rep, fsdp, None),
        P(rep, fsdp, None),
        P(rep, fsdp, None),
        P(rep),
        P(fsdp, rep),
        P(fsdp, rep),
    )
    return jax.shard_map(
        local,
        mesh=split,
        in_specs=placed,
        out_specs=(P(fsdp, rep), P(fsdp, rep), P(fsdp, None)),
        check_vma=False,
    )
```

```python
import functools

import jax
import jax.numpy as jnp
from jax import lax
from jax.experimental import pallas as pl
from jax.experimental.pallas import tpu as pltpu
from jax.sharding import Mesh
from jax.sharding import PartitionSpec as P

ROUND = 3
MESH = pl.DeviceIdType.MESH
CHUNKS = (64, 128, 128, 128, 128, 128, 128, 64)
READY = {"multiply": 0, "merge": 1.01, "along_z": 2.02, "finish": 3.03, "gather_y": 4.04, "pass_y": 5.05, "deliver": 6.06}
AHEAD = 2
RELAY = (0, 1, 2, 3, 4, 5)
Y_FIRST = ()
F32 = jnp.float32
BF16 = jnp.bfloat16


def kernel(
    p_ref, h_ref, g_ref, n_ref, z_ref, x_ref,
    zo_ref, xo_ref, yo_ref,
    hb, at, ab, gb, pb, wp, cb, r1a, r1b, r2a, r2b, zs, yg, zt, xt, zf, xf, nzt, nxt, wt, ty, tz,
    in_sem, b_send, b_recv, sib_send, sib_recv, a_send, a_recv,
    y1_send, y1_recv, y2_send, y2_recv, z_send, z_recv, g1_send, g1_recv, g2_send, g2_recv,
    o_send, o_recv, t_send, t_recv, e_send, e_recv,
):
    x, y, c = lax.axis_index("x"), lax.axis_index("y"), lax.axis_index("c")
    zh, zl = lax.axis_index("zh"), lax.axis_index("zl")
    z = zh * 4 + zl
    owner = zh == c
    other = 1 - c

    def plus(v, d, n=4):
        return lax.rem(v + d, n)

    def rdma(src, dst, ss, rs, **where):
        return pltpu.make_async_remote_copy(
            src_ref=src, dst_ref=dst, send_sem=ss, recv_sem=rs, device_id=where, device_id_type=MESH
        )

    def await_bytes(ref, sem):
        pltpu.make_async_copy(ref, ref, sem).wait()

    starts = [sum(CHUNKS[:m]) for m in range(len(CHUNKS))]
    rows_of = [slice(s, s + r) for s, r in zip(starts, CHUNKS)]
    n_chunks = len(CHUNKS)

    g_in = pltpu.make_async_copy(g_ref, gb.at[0, pl.ds(0, 128)], in_sem.at[0])
    g_in.start()
    h_in = pltpu.make_async_copy(h_ref, hb, in_sem.at[1])
    h_in.start()
    mine = pl.ds(pl.multiple_of(c * 64, 64), 64)
    theirs = pl.ds(pl.multiple_of(other * 64, 64), 64)
    z_in = pltpu.make_async_copy(z_ref, zt.at[mine], in_sem.at[2])
    z_in.start()
    x_in = pltpu.make_async_copy(x_ref, xt.at[mine], in_sem.at[3])
    x_in.start()
    p_in = pltpu.make_async_copy(p_ref, pb.at[0], in_sem.at[4])

    @pl.when(owner)
    def _():
        p_in.start()

    wt[0] = jnp.full((8, 128), n_ref[0].astype(F32), F32)

    barrier = pltpu.get_barrier_semaphore()
    peers = [{"zh": plus(z, d, 8) // 4, "zl": plus(z, d, 4)} for d in (4, 3, 5, 2, 6, 1, 7)]
    peers += [{"x": plus(x, d), "c": k} for d in (1, 2, 3) for k in (c, other)]
    peers += [{"y": plus(y, d)} for d in (1, 2, 3)]
    peers += [{"c": other}]
    for peer in peers:
        pl.semaphore_signal(barrier, inc=1, device_id=peer, device_id_type=MESH)
    pl.semaphore_wait(barrier, len(peers))

    xp, xm = plus(x, 1), plus(x, 3)
    g_in.wait()
    lo, hi = pl.ds(0, 64), pl.ds(64, 64)
    own_lo, own_hi = gb.at[0, pl.ds(0, 64)], gb.at[0, pl.ds(64, 64)]
    from_left = [gb.at[0, pl.ds(128, 64)], gb.at[0, pl.ds(192, 64)]]
    from_right = [gb.at[0, pl.ds(384, 64)], gb.at[0, pl.ds(448, 64)]]
    far = [gb.at[0, pl.ds(256, 64)], gb.at[0, pl.ds(320, 64)]]
    b_copies = [
        rdma(own_lo, from_left[0], b_send.at[0], b_recv.at[0], x=xp),
        rdma(own_hi, from_right[1], b_send.at[3], b_recv.at[3], x=xm),
        rdma(own_hi, from_left[1], b_send.at[1], b_recv.at[1], x=xp),
        rdma(own_lo, from_right[0], b_send.at[2], b_recv.at[2], x=xm),
    ]
    for copy in b_copies[:2]:
        copy.start()

    def to_sibling(k):
        part = pl.ds(k * 128, 128)
        return rdma(gb.at[0, part], gb.at[1, part], sib_send.at[k], sib_recv.at[k], c=other)

    w_copy = rdma(wt.at[0], wt.at[1], e_send.at[0], e_recv.at[0], c=other)
    w_copy.start()
    sib_copies = [to_sibling(k) for k in range(4)]
    sib_copies[0].start()
    p_copy = rdma(p_ref, pb.at[1], e_send.at[1], e_recv.at[1], c=other)

    @pl.when(jnp.logical_not(owner))
    def _():
        p_copy.start()

    z_copy = rdma(z_ref, zt.at[mine], e_send.at[2], e_recv.at[2], c=other)
    z_copy.start()
    x_copy = rdma(x_ref, xt.at[mine], e_send.at[3], e_recv.at[3], c=other)
    x_copy.start()

    h_in.wait()

    def transpose(q):
        for i in range(7):
            cols = pl.ds(pl.multiple_of(q * 896 + i * 128, 128), 128)
            at[q, i * 128 : (i + 1) * 128, :] = hb[:, cols].T

    pl.loop(0, 3)(transpose)
    for copy in b_copies[2:]:
        copy.start()
    pl.loop(3, 8)(transpose)

    w_copy.wait()
    ty[0] = wt[0] + wt[1]
    ty_copies = [rdma(ty.at[0], ty.at[d], t_send.at[d - 1], t_recv.at[d - 1], y=plus(y, d)) for d in (1, 2, 3)]
    for copy in ty_copies:
        copy.start()

    def send_inputs(m):
        r = rows_of[m]
        for dx in (2, 1, 3, 0):
            for dc in (0, 1):
                core = plus(c, dc, 2)
                to_x = plus(x, dx)
                src = at.at[core * 4 + to_x, r]
                dst = ab.at[r, pl.ds((dc * 4 + dx) * 128, 128)]
                if dx == 0 and dc == 0:
                    pltpu.make_async_copy(src, dst, a_recv.at[m]).start()
                else:
                    rdma(src, dst, a_send.at[m], a_recv.at[m], x=to_x, c=core).start()

    b_copies[0].wait_recv()
    fwd_a = rdma(from_left[0], far[0], b_send.at[4], b_recv.at[4], x=xp)
    fwd_a.start()
    b_copies[1].wait_recv()
    fwd_b = rdma(from_right[1], far[1], b_send.at[5], b_recv.at[5], x=xm)
    fwd_b.start()

    for copy in ty_copies:
        copy.wait()
    tz[0] = ty[0] + ty[1] + ty[2] + ty[3]
    tz_copies = [rdma(tz.at[0], tz.at[d], t_send.at[d + 2], t_recv.at[d + 2], zl=plus(zl, d)) for d in (1, 2, 3)]
    for copy in tz_copies:
        copy.start()

    w_own, w_sib = wt[0][0:1, :], wt[1][0:1, :]

    @pl.when(owner)
    def _():
        p_in.wait()
        p_copy.wait_recv()

        @pl.loop(0, 56)
        def _(i):
            r = pl.ds(pl.multiple_of(i * 16, 16), 16)
            for j in range(16):
                k = slice(j * 128, (j + 1) * 128)
                wp[r, k] = w_own * pb[0, r, k].astype(F32) + w_sib * pb[1, r, k].astype(F32)

    @pl.when(jnp.logical_not(owner))
    def _():
        p_copy.wait_send()

        @pl.loop(0, 56)
        def _(i):
            r = pl.ds(pl.multiple_of(i * 16, 16), 16)
            wp[r, :] = jnp.zeros((16, 2048), F32)

    z_in.wait()
    x_in.wait()
    z_copy.wait()
    x_copy.wait()
    for i in range(7):
        k = slice(i * 128, (i + 1) * 128)
        zf[k, :] = zt[:, k].T
        xf[k, :] = xt[:, k].T
    for copy in tz_copies:
        copy.wait()
    total = (tz[0] + tz[1] + tz[2] + tz[3])[0:1, :]

    b_copies[2].wait_recv()
    sib_copies[1].start()
    b_copies[3].wait_recv()
    sib_copies[3].start()
    send_inputs(0)
    fwd_a.wait_recv()
    fwd_b.wait_recv()
    sib_copies[2].start()
    for m in range(1, AHEAD):
        send_inputs(m)
    for copy in sib_copies:
        copy.wait_recv()

    yp, ym, yf = plus(y, 1), plus(y, 3), plus(y, 2)

    def y_first(m):
        r = rows_of[m]
        return [
            rdma(cb.at[yf, pl.ds(0, 2), r], r1a.at[:, r], y1_send.at[m, 0], y1_recv.at[m, 0], y=yp),
            rdma(cb.at[yf, pl.ds(2, 2), r], r1b.at[:, r], y1_send.at[m, 1], y1_recv.at[m, 1], y=ym),
        ]

    def y_second(m):
        r = rows_of[m]
        return [
            rdma(cb.at[yp, :, r], r2a.at[:, r], y2_send.at[m, 0], y2_recv.at[m, 0], y=yp),
            rdma(cb.at[ym, :, r], r2b.at[:, r], y2_send.at[m, 1], y2_recv.at[m, 1], y=ym),
        ]

    def multiply(m):
        r = rows_of[m]
        await_bytes(ab.at[r], a_recv.at[m])
        if m + AHEAD < n_chunks:
            send_inputs(m + AHEAD)

        @pl.loop(0, 4)
        def _(q):
            cols = pl.ds(pl.multiple_of(q * 512, 512), 512)
            d_own = jnp.dot(ab[r, 0:512], gb[0, :, cols], preferred_element_type=F32)
            d_sib = jnp.dot(ab[r, 512:1024], gb[1, :, cols], preferred_element_type=F32)
            for j in range(4):
                k = slice(j * 128, (j + 1) * 128)
                base = wp[r, pl.ds(pl.multiple_of(q * 512 + j * 128, 128), 128)]
                cb[j, q, r] = (base - 0.1 * (w_own * d_own[:, k] + w_sib * d_sib[:, k])).astype(BF16)

        for copy in y_first(m):
            copy.start()

    def merge(m):
        r = rows_of[m]
        first, second = y_first(m), y_second(m)
        first[0].wait_recv()
        for j in (0, 1):
            cb[yp, j, r] = (cb[yp, j, r].astype(F32) + r1a[j, r].astype(F32)).astype(BF16)
        second[0].start()
        first[1].wait_recv()
        for j in (2, 3):
            cb[ym, j, r] = (cb[ym, j, r].astype(F32) + r1b[j - 2, r].astype(F32)).astype(BF16)
        second[1].start()

    def z_copies(m):
        r = rows_of[m]
        return [
            rdma(cb.at[y, plus(zl, d), r], zs.at[z, r], z_send.at[m], z_recv.at[m], zh=c, zl=plus(zl, d))
            for d in range(4)
        ]

    def along_z(m):
        r = rows_of[m]
        for copy in y_second(m):
            copy.wait_recv()
        for j in range(4):
            cb[y, j, r] = (cb[y, j, r].astype(F32) + r2a[j, r].astype(F32) + r2b[j, r].astype(F32)).astype(BF16)
        copies = z_copies(m)
        for d in (2, 1, 3):
            copies[d].start()

        @pl.when(owner)
        def _():
            pltpu.make_async_copy(cb.at[y, zl, r], zs.at[z, r], z_recv.at[m]).start()

        @pl.when(jnp.logical_not(owner))
        def _():
            copies[0].start()

    def finish(m):
        r = rows_of[m]
        await_bytes(zs.at[:, r], z_recv.at[m])
        summed = zs[0, r].astype(F32)
        for k in range(1, 8):
            summed = summed + zs[k, r].astype(F32)
        outer_z, outer_x = zf[r, :], xf[r, :]
        anchor = 0.1 * outer_z + 0.9 * outer_x
        pseudo = anchor - summed / total
        new_z = outer_z - 0.7 * pseudo
        mixing = 1.0 / (ROUND + 1.0)
        new_x = (1.0 - mixing) * outer_x + mixing * new_z
        yg[y, zl, r] = (0.1 * new_z + 0.9 * new_x).astype(BF16)
        for d in (2, 1, 3):
            where = {"y": plus(y, d)} if m in Y_FIRST else {"zl": plus(zl, d)}
            rdma(yg.at[y, zl, r], yg.at[y, zl, r], g1_send.at[m], g1_recv.at[m], **where).start()
        zf[r, :] = new_z
        xf[r, :] = new_x

    def gather_y(m):
        r = rows_of[m]
        await_bytes(yg.at[y, pl.ds(0, 3), r], g1_recv.at[m])
        if m in Y_FIRST:
            part, steps = yg.at[:, zl, r], [({"zl": plus(zl, d)}, 0) for d in (2, 1, 3)]
        elif m in RELAY:
            part, steps = yg.at[y, :, r], [({"y": yp}, 0), ({"y": ym}, 1)]
        else:
            part, steps = yg.at[y, :, r], [({"y": plus(y, d)}, 0) for d in (2, 1, 3)]
        for where, k in steps:
            rdma(part, part, g2_send.at[m], g2_recv.at[m, k], **where).start()

    def pass_y(m):
        r = rows_of[m]
        await_bytes(yg.at[ym, :, r], g2_recv.at[m, 0])
        part = yg.at[ym, pl.ds(0, 2), r]
        rdma(part, part, g2_send.at[m], g2_recv.at[m, 2], y=yp).start()
        await_bytes(yg.at[yp, :, r], g2_recv.at[m, 1])
        part = yg.at[yp, pl.ds(2, 2), r]
        rdma(part, part, g2_send.at[m], g2_recv.at[m, 3], y=ym).start()

    def out_away(m):
        r = rows_of[m]
        return rdma(yo_ref.at[r], yo_ref.at[r], o_send.at[m], o_recv.at[m], c=other)

    def deliver(m):
        r = rows_of[m]
        if m in RELAY:
            await_bytes(yg.at[yf, pl.ds(0, 2), r], g2_recv.at[m, 2])
            await_bytes(yg.at[yf, pl.ds(2, 2), r], g2_recv.at[m, 3])
        else:
            await_bytes(yg.at[pl.ds(0, 3), :, r], g2_recv.at[m, 0])
        for j in range(16):
            yo_ref[r, j * 128 : (j + 1) * 128] = yg[j % 4, j // 4, r]
        out_away(m).start()

    state_out = (
        pltpu.make_async_copy(nzt.at[mine], zo_ref, in_sem.at[5]),
        pltpu.make_async_copy(nxt.at[mine], xo_ref, in_sem.at[6]),
    )
    state_away = (
        rdma(nzt.at[theirs], zo_ref, e_send.at[4], e_recv.at[4], c=other),
        rdma(nxt.at[theirs], xo_ref, e_send.at[5], e_recv.at[5], c=other),
    )

    def state(m):
        for i in range(7):
            k = slice(i * 128, (i + 1) * 128)
            nzt[:, k] = zf[k, :].T
            nxt[:, k] = xf[k, :].T
        for copy in (*state_out, *state_away):
            copy.start()

    stages = {
        "multiply": multiply, "merge": merge, "along_z": along_z,
        "finish": finish, "gather_y": gather_y, "pass_y": pass_y, "deliver": deliver,
    }
    order = sorted(
        (starts[m] / 128 + ready, k, m)
        for m in range(n_chunks)
        for k, (stage, ready) in enumerate(READY.items())
        if stage != "pass_y" or m in RELAY
    )
    names = list(READY)
    for _, k, m in order:
        if k < 3:
            stages[names[k]](m)
        else:

            @pl.when(owner)
            def _():
                stages[names[k]](m)
                if names[k] == "finish" and m == n_chunks - 1:
                    state(m)

    for copy in (*b_copies, fwd_a, fwd_b, *sib_copies):
        copy.wait_send()
    for m in range(n_chunks):
        r = rows_of[m]
        await_bytes(ab.at[r, pl.ds(0, 896)], a_send.at[m])
        for copy in (*y_first(m), *y_second(m)):
            copy.wait_send()

    @pl.when(owner)
    def _():
        for m in range(n_chunks):
            r = rows_of[m]
            await_bytes(zs.at[pl.ds(0, 3), r], z_send.at[m])
            await_bytes(yg.at[0, pl.ds(0, 3), r], g1_send.at[m])
            await_bytes(yg.at[pl.ds(0, 3), :, r], g2_send.at[m])
            out_away(m).wait_send()
        for copy in state_out:
            copy.wait()
        for copy in state_away:
            copy.wait_send()

    @pl.when(jnp.logical_not(owner))
    def _():
        for m in range(n_chunks):
            await_bytes(zs.at[pl.ds(0, 4), rows_of[m]], z_send.at[m])
            out_away(m).wait_recv()
        for copy in state_away:
            copy.wait_recv()


def local(params, hidden_acts, out_grads, step_counts, outer_z, outer_x):
    n = len(CHUNKS)
    dma = pltpu.SemaphoreType.DMA
    hbm = pl.BlockSpec(memory_space=pl.ANY)
    vmem = pl.BlockSpec(memory_space=pltpu.VMEM)
    new_z, new_x, new_y = pl.pallas_call(
        kernel,
        name="outer_sync",
        out_shape=(pltpu.VMEM((64, 896), F32), pltpu.VMEM((64, 896), F32), pltpu.VMEM((896, 2048), BF16)),
        in_specs=[hbm, hbm, hbm, pl.BlockSpec(memory_space=pltpu.SMEM), hbm, hbm],
        out_specs=(vmem, vmem, vmem),
        scratch_shapes=[
            pltpu.VMEM((128, 7168), BF16),
            pltpu.VMEM((8, 896, 128), BF16),
            pltpu.VMEM((896, 1024), BF16),
            pltpu.VMEM((2, 512, 2048), BF16),
            pltpu.VMEM((2, 896, 2048), BF16),
            pltpu.VMEM((896, 2048), F32),
            pltpu.VMEM((4, 4, 896, 128), BF16),
            pltpu.VMEM((2, 896, 128), BF16),
            pltpu.VMEM((2, 896, 128), BF16),
            pltpu.VMEM((4, 896, 128), BF16),
            pltpu.VMEM((4, 896, 128), BF16),
            pltpu.VMEM((8, 896, 128), BF16),
            pltpu.VMEM((4, 4, 896, 128), BF16),
            pltpu.VMEM((128, 896), F32),
            pltpu.VMEM((128, 896), F32),
            pltpu.VMEM((896, 128), F32),
            pltpu.VMEM((896, 128), F32),
            pltpu.VMEM((128, 896), F32),
            pltpu.VMEM((128, 896), F32),
            pltpu.VMEM((2, 8, 128), F32),
            pltpu.VMEM((4, 8, 128), F32),
            pltpu.VMEM((4, 8, 128), F32),
            dma((7,)),
            dma((6,)), dma((6,)),
            dma((4,)), dma((4,)),
            dma((n,)), dma((n,)),
            dma((n, 2)), dma((n, 2)),
            dma((n, 2)), dma((n, 2)),
            dma((n,)), dma((n,)),
            dma((n,)), dma((n,)),
            dma((n,)), dma((n, 4)),
            dma((n,)), dma((n,)),
            dma((6,)), dma((6,)),
            dma((6,)), dma((6,)),
        ],
        compiler_params=pltpu.CompilerParams(
            collective_id=0, has_side_effects=True, vmem_limit_bytes=50 * 2**20
        ),
        cost_estimate=pl.CostEstimate(flops=3_760_000_000, bytes_accessed=12_000_000, transcendentals=0),
    )(params[0], hidden_acts[0], out_grads[0], step_counts, outer_z.T, outer_x.T)
    return new_z.T, new_x.T, new_y


def solution(mesh):
    split = Mesh(mesh.devices.reshape(4, 4, 2, 2, 4), ("zl", "y", "c", "zh", "x"))
    rep, fsdp = ("zl", "y", "c"), ("zh", "x")
    placed = (
        P(rep, fsdp, None),
        P(rep, fsdp, None),
        P(rep, fsdp, None),
        P(rep),
        P(fsdp, rep),
        P(fsdp, rep),
    )
    return jax.shard_map(
        local,
        mesh=split,
        in_specs=placed,
        out_specs=(P(fsdp, rep), P(fsdp, rep), P(fsdp, None)),
        check_vma=False,
    )
```

```python
import functools

import jax
import jax.numpy as jnp
from jax import lax
from jax.experimental import pallas as pl
from jax.experimental.pallas import tpu as pltpu
from jax.sharding import Mesh
from jax.sharding import PartitionSpec as P

ROUND = 3
MESH = pl.DeviceIdType.MESH
CHUNKS = (64, 64, 128, 128, 128, 128, 128, 64, 64)
READY = {"multiply": 0, "merge": 1.01, "along_z": 2.02, "finish": 3.03, "gather_y": 4.04, "pass_y": 5.05, "deliver": 6.06}
AHEAD = 2
RELAY = (0, 1, 2, 3, 4, 5, 6)
Y_FIRST = ()
F32 = jnp.float32
BF16 = jnp.bfloat16


def kernel(
    p_ref, h_ref, g_ref, n_ref, z_ref, x_ref,
    zo_ref, xo_ref, yo_ref,
    hb, at, ab, gb, pb, wp, cb, r1a, r1b, r2a, r2b, zs, yg, zt, xt, zf, xf, nzt, nxt, wt, ty, tz,
    in_sem, b_send, b_recv, sib_send, sib_recv, a_send, a_recv,
    y1_send, y1_recv, y2_send, y2_recv, z_send, z_recv, g1_send, g1_recv, g2_send, g2_recv,
    o_send, o_recv, t_send, t_recv, e_send, e_recv,
):
    x, y, c = lax.axis_index("x"), lax.axis_index("y"), lax.axis_index("c")
    zh, zl = lax.axis_index("zh"), lax.axis_index("zl")
    z = zh * 4 + zl
    owner = zh == c
    other = 1 - c

    def plus(v, d, n=4):
        return lax.rem(v + d, n)

    def rdma(src, dst, ss, rs, **where):
        return pltpu.make_async_remote_copy(
            src_ref=src, dst_ref=dst, send_sem=ss, recv_sem=rs, device_id=where, device_id_type=MESH
        )

    def await_bytes(ref, sem):
        pltpu.make_async_copy(ref, ref, sem).wait()

    starts = [sum(CHUNKS[:m]) for m in range(len(CHUNKS))]
    rows_of = [slice(s, s + r) for s, r in zip(starts, CHUNKS)]
    n_chunks = len(CHUNKS)

    g_in = pltpu.make_async_copy(g_ref, gb.at[0, pl.ds(0, 128)], in_sem.at[0])
    g_in.start()
    h_in = pltpu.make_async_copy(h_ref, hb, in_sem.at[1])
    h_in.start()
    mine = pl.ds(pl.multiple_of(c * 64, 64), 64)
    theirs = pl.ds(pl.multiple_of(other * 64, 64), 64)
    z_in = pltpu.make_async_copy(z_ref, zt.at[mine], in_sem.at[2])
    z_in.start()
    x_in = pltpu.make_async_copy(x_ref, xt.at[mine], in_sem.at[3])
    x_in.start()
    p_in = pltpu.make_async_copy(p_ref, pb.at[0], in_sem.at[4])

    @pl.when(owner)
    def _():
        p_in.start()

    wt[0] = jnp.full((8, 128), n_ref[0].astype(F32), F32)

    barrier = pltpu.get_barrier_semaphore()
    peers = [{"zh": plus(z, d, 8) // 4, "zl": plus(z, d, 4)} for d in (4, 3, 5, 2, 6, 1, 7)]
    peers += [{"x": plus(x, d), "c": k} for d in (1, 2, 3) for k in (c, other)]
    peers += [{"y": plus(y, d)} for d in (1, 2, 3)]
    peers += [{"c": other}]
    for peer in peers:
        pl.semaphore_signal(barrier, inc=1, device_id=peer, device_id_type=MESH)
    pl.semaphore_wait(barrier, len(peers))

    xp, xm = plus(x, 1), plus(x, 3)
    g_in.wait()
    lo, hi = pl.ds(0, 64), pl.ds(64, 64)
    own_lo, own_hi = gb.at[0, pl.ds(0, 64)], gb.at[0, pl.ds(64, 64)]
    from_left = [gb.at[0, pl.ds(128, 64)], gb.at[0, pl.ds(192, 64)]]
    from_right = [gb.at[0, pl.ds(384, 64)], gb.at[0, pl.ds(448, 64)]]
    far = [gb.at[0, pl.ds(256, 64)], gb.at[0, pl.ds(320, 64)]]
    b_copies = [
        rdma(own_lo, from_left[0], b_send.at[0], b_recv.at[0], x=xp),
        rdma(own_hi, from_right[1], b_send.at[3], b_recv.at[3], x=xm),
        rdma(own_hi, from_left[1], b_send.at[1], b_recv.at[1], x=xp),
        rdma(own_lo, from_right[0], b_send.at[2], b_recv.at[2], x=xm),
    ]
    for copy in b_copies[:2]:
        copy.start()

    def to_sibling(k):
        part = pl.ds(k * 128, 128)
        return rdma(gb.at[0, part], gb.at[1, part], sib_send.at[k], sib_recv.at[k], c=other)

    w_copy = rdma(wt.at[0], wt.at[1], e_send.at[0], e_recv.at[0], c=other)
    w_copy.start()
    sib_copies = [to_sibling(k) for k in range(4)]
    sib_copies[0].start()
    p_copy = rdma(p_ref, pb.at[1], e_send.at[1], e_recv.at[1], c=other)

    @pl.when(jnp.logical_not(owner))
    def _():
        p_copy.start()

    z_copy = rdma(z_ref, zt.at[mine], e_send.at[2], e_recv.at[2], c=other)
    z_copy.start()
    x_copy = rdma(x_ref, xt.at[mine], e_send.at[3], e_recv.at[3], c=other)
    x_copy.start()

    h_in.wait()

    def transpose(q):
        for i in range(7):
            cols = pl.ds(pl.multiple_of(q * 896 + i * 128, 128), 128)
            at[q, i * 128 : (i + 1) * 128, :] = hb[:, cols].T

    pl.loop(0, 3)(transpose)
    for copy in b_copies[2:]:
        copy.start()
    pl.loop(3, 8)(transpose)

    w_copy.wait()
    ty[0] = wt[0] + wt[1]
    ty_copies = [rdma(ty.at[0], ty.at[d], t_send.at[d - 1], t_recv.at[d - 1], y=plus(y, d)) for d in (1, 2, 3)]
    for copy in ty_copies:
        copy.start()

    def send_inputs(m):
        r = rows_of[m]
        for dx in (2, 1, 3, 0):
            for dc in (0, 1):
                core = plus(c, dc, 2)
                to_x = plus(x, dx)
                src = at.at[core * 4 + to_x, r]
                dst = ab.at[r, pl.ds((dc * 4 + dx) * 128, 128)]
                if dx == 0 and dc == 0:
                    pltpu.make_async_copy(src, dst, a_recv.at[m]).start()
                else:
                    rdma(src, dst, a_send.at[m], a_recv.at[m], x=to_x, c=core).start()

    b_copies[0].wait_recv()
    fwd_a = rdma(from_left[0], far[0], b_send.at[4], b_recv.at[4], x=xp)
    fwd_a.start()
    b_copies[1].wait_recv()
    fwd_b = rdma(from_right[1], far[1], b_send.at[5], b_recv.at[5], x=xm)
    fwd_b.start()

    for copy in ty_copies:
        copy.wait()
    tz[0] = ty[0] + ty[1] + ty[2] + ty[3]
    tz_copies = [rdma(tz.at[0], tz.at[d], t_send.at[d + 2], t_recv.at[d + 2], zl=plus(zl, d)) for d in (1, 2, 3)]
    for copy in tz_copies:
        copy.start()

    w_own, w_sib = wt[0][0:1, :], wt[1][0:1, :]

    @pl.when(owner)
    def _():
        p_in.wait()
        p_copy.wait_recv()

        @pl.loop(0, 56)
        def _(i):
            r = pl.ds(pl.multiple_of(i * 16, 16), 16)
            for j in range(16):
                k = slice(j * 128, (j + 1) * 128)
                wp[r, k] = w_own * pb[0, r, k].astype(F32) + w_sib * pb[1, r, k].astype(F32)

    @pl.when(jnp.logical_not(owner))
    def _():
        p_copy.wait_send()

        @pl.loop(0, 56)
        def _(i):
            r = pl.ds(pl.multiple_of(i * 16, 16), 16)
            wp[r, :] = jnp.zeros((16, 2048), F32)

    z_in.wait()
    x_in.wait()
    z_copy.wait()
    x_copy.wait()
    for i in range(7):
        k = slice(i * 128, (i + 1) * 128)
        zf[k, :] = zt[:, k].T
        xf[k, :] = xt[:, k].T
    for copy in tz_copies:
        copy.wait()
    total = (tz[0] + tz[1] + tz[2] + tz[3])[0:1, :]

    b_copies[2].wait_recv()
    sib_copies[1].start()
    b_copies[3].wait_recv()
    sib_copies[3].start()
    send_inputs(0)
    fwd_a.wait_recv()
    fwd_b.wait_recv()
    sib_copies[2].start()
    for m in range(1, AHEAD):
        send_inputs(m)
    for copy in sib_copies:
        copy.wait_recv()

    yp, ym, yf = plus(y, 1), plus(y, 3), plus(y, 2)

    def y_first(m):
        r = rows_of[m]
        return [
            rdma(cb.at[yf, pl.ds(0, 2), r], r1a.at[:, r], y1_send.at[m, 0], y1_recv.at[m, 0], y=yp),
            rdma(cb.at[yf, pl.ds(2, 2), r], r1b.at[:, r], y1_send.at[m, 1], y1_recv.at[m, 1], y=ym),
        ]

    def y_second(m):
        r = rows_of[m]
        return [
            rdma(cb.at[yp, :, r], r2a.at[:, r], y2_send.at[m, 0], y2_recv.at[m, 0], y=yp),
            rdma(cb.at[ym, :, r], r2b.at[:, r], y2_send.at[m, 1], y2_recv.at[m, 1], y=ym),
        ]

    def multiply(m):
        r = rows_of[m]
        await_bytes(ab.at[r], a_recv.at[m])
        if m + AHEAD < n_chunks:
            send_inputs(m + AHEAD)

        @pl.loop(0, 4)
        def _(q):
            cols = pl.ds(pl.multiple_of(q * 512, 512), 512)
            d_own = jnp.dot(ab[r, 0:512], gb[0, :, cols], preferred_element_type=F32)
            d_sib = jnp.dot(ab[r, 512:1024], gb[1, :, cols], preferred_element_type=F32)
            for j in range(4):
                k = slice(j * 128, (j + 1) * 128)
                base = wp[r, pl.ds(pl.multiple_of(q * 512 + j * 128, 128), 128)]
                cb[j, q, r] = (base - 0.1 * (w_own * d_own[:, k] + w_sib * d_sib[:, k])).astype(BF16)

        for copy in y_first(m):
            copy.start()

    def merge(m):
        r = rows_of[m]
        first, second = y_first(m), y_second(m)
        first[0].wait_recv()
        for j in (0, 1):
            cb[yp, j, r] = (cb[yp, j, r].astype(F32) + r1a[j, r].astype(F32)).astype(BF16)
        second[0].start()
        first[1].wait_recv()
        for j in (2, 3):
            cb[ym, j, r] = (cb[ym, j, r].astype(F32) + r1b[j - 2, r].astype(F32)).astype(BF16)
        second[1].start()

    def z_copies(m):
        r = rows_of[m]
        return [
            rdma(cb.at[y, plus(zl, d), r], zs.at[z, r], z_send.at[m], z_recv.at[m], zh=c, zl=plus(zl, d))
            for d in range(4)
        ]

    def along_z(m):
        r = rows_of[m]
        for copy in y_second(m):
            copy.wait_recv()
        for j in range(4):
            cb[y, j, r] = (cb[y, j, r].astype(F32) + r2a[j, r].astype(F32) + r2b[j, r].astype(F32)).astype(BF16)
        copies = z_copies(m)
        for d in (2, 1, 3):
            copies[d].start()

        @pl.when(owner)
        def _():
            pltpu.make_async_copy(cb.at[y, zl, r], zs.at[z, r], z_recv.at[m]).start()

        @pl.when(jnp.logical_not(owner))
        def _():
            copies[0].start()

    def finish(m):
        r = rows_of[m]
        await_bytes(zs.at[:, r], z_recv.at[m])
        summed = zs[0, r].astype(F32)
        for k in range(1, 8):
            summed = summed + zs[k, r].astype(F32)
        outer_z, outer_x = zf[r, :], xf[r, :]
        anchor = 0.1 * outer_z + 0.9 * outer_x
        pseudo = anchor - summed / total
        new_z = outer_z - 0.7 * pseudo
        mixing = 1.0 / (ROUND + 1.0)
        new_x = (1.0 - mixing) * outer_x + mixing * new_z
        yg[y, zl, r] = (0.1 * new_z + 0.9 * new_x).astype(BF16)
        for d in (2, 1, 3):
            where = {"y": plus(y, d)} if m in Y_FIRST else {"zl": plus(zl, d)}
            rdma(yg.at[y, zl, r], yg.at[y, zl, r], g1_send.at[m], g1_recv.at[m], **where).start()
        zf[r, :] = new_z
        xf[r, :] = new_x

    def gather_y(m):
        r = rows_of[m]
        await_bytes(yg.at[y, pl.ds(0, 3), r], g1_recv.at[m])
        if m in Y_FIRST:
            part, steps = yg.at[:, zl, r], [({"zl": plus(zl, d)}, 0) for d in (2, 1, 3)]
        elif m in RELAY:
            part, steps = yg.at[y, :, r], [({"y": yp}, 0), ({"y": ym}, 1)]
        else:
            part, steps = yg.at[y, :, r], [({"y": plus(y, d)}, 0) for d in (2, 1, 3)]
        for where, k in steps:
            rdma(part, part, g2_send.at[m], g2_recv.at[m, k], **where).start()

    def pass_y(m):
        r = rows_of[m]
        await_bytes(yg.at[ym, :, r], g2_recv.at[m, 0])
        part = yg.at[ym, pl.ds(0, 2), r]
        rdma(part, part, g2_send.at[m], g2_recv.at[m, 2], y=yp).start()
        await_bytes(yg.at[yp, :, r], g2_recv.at[m, 1])
        part = yg.at[yp, pl.ds(2, 2), r]
        rdma(part, part, g2_send.at[m], g2_recv.at[m, 3], y=ym).start()

    def out_away(m):
        r = rows_of[m]
        return rdma(yo_ref.at[r], yo_ref.at[r], o_send.at[m], o_recv.at[m], c=other)

    def deliver(m):
        r = rows_of[m]
        if m in RELAY:
            await_bytes(yg.at[yf, pl.ds(0, 2), r], g2_recv.at[m, 2])
            await_bytes(yg.at[yf, pl.ds(2, 2), r], g2_recv.at[m, 3])
        else:
            await_bytes(yg.at[pl.ds(0, 3), :, r], g2_recv.at[m, 0])
        for j in range(16):
            yo_ref[r, j * 128 : (j + 1) * 128] = yg[j % 4, j // 4, r]
        out_away(m).start()

    state_out = (
        pltpu.make_async_copy(nzt.at[mine], zo_ref, in_sem.at[5]),
        pltpu.make_async_copy(nxt.at[mine], xo_ref, in_sem.at[6]),
    )
    state_away = (
        rdma(nzt.at[theirs], zo_ref, e_send.at[4], e_recv.at[4], c=other),
        rdma(nxt.at[theirs], xo_ref, e_send.at[5], e_recv.at[5], c=other),
    )

    def state(m):
        for i in range(7):
            k = slice(i * 128, (i + 1) * 128)
            nzt[:, k] = zf[k, :].T
            nxt[:, k] = xf[k, :].T
        for copy in (*state_out, *state_away):
            copy.start()

    stages = {
        "multiply": multiply, "merge": merge, "along_z": along_z,
        "finish": finish, "gather_y": gather_y, "pass_y": pass_y, "deliver": deliver,
    }
    order = sorted(
        (starts[m] / 128 + ready, k, m)
        for m in range(n_chunks)
        for k, (stage, ready) in enumerate(READY.items())
        if stage != "pass_y" or m in RELAY
    )
    names = list(READY)
    for _, k, m in order:
        if k < 3:
            stages[names[k]](m)
        else:

            @pl.when(owner)
            def _():
                stages[names[k]](m)
                if names[k] == "finish" and m == n_chunks - 1:
                    state(m)

    for copy in (*b_copies, fwd_a, fwd_b, *sib_copies):
        copy.wait_send()
    for m in range(n_chunks):
        r = rows_of[m]
        await_bytes(ab.at[r, pl.ds(0, 896)], a_send.at[m])
        for copy in (*y_first(m), *y_second(m)):
            copy.wait_send()

    @pl.when(owner)
    def _():
        for m in range(n_chunks):
            r = rows_of[m]
            await_bytes(zs.at[pl.ds(0, 3), r], z_send.at[m])
            await_bytes(yg.at[0, pl.ds(0, 3), r], g1_send.at[m])
            await_bytes(yg.at[pl.ds(0, 3), :, r], g2_send.at[m])
            out_away(m).wait_send()
        for copy in state_out:
            copy.wait()
        for copy in state_away:
            copy.wait_send()

    @pl.when(jnp.logical_not(owner))
    def _():
        for m in range(n_chunks):
            await_bytes(zs.at[pl.ds(0, 4), rows_of[m]], z_send.at[m])
            out_away(m).wait_recv()
        for copy in state_away:
            copy.wait_recv()


def local(params, hidden_acts, out_grads, step_counts, outer_z, outer_x):
    n = len(CHUNKS)
    dma = pltpu.SemaphoreType.DMA
    hbm = pl.BlockSpec(memory_space=pl.ANY)
    vmem = pl.BlockSpec(memory_space=pltpu.VMEM)
    new_z, new_x, new_y = pl.pallas_call(
        kernel,
        name="outer_sync",
        out_shape=(pltpu.VMEM((64, 896), F32), pltpu.VMEM((64, 896), F32), pltpu.VMEM((896, 2048), BF16)),
        in_specs=[hbm, hbm, hbm, pl.BlockSpec(memory_space=pltpu.SMEM), hbm, hbm],
        out_specs=(vmem, vmem, vmem),
        scratch_shapes=[
            pltpu.VMEM((128, 7168), BF16),
            pltpu.VMEM((8, 896, 128), BF16),
            pltpu.VMEM((896, 1024), BF16),
            pltpu.VMEM((2, 512, 2048), BF16),
            pltpu.VMEM((2, 896, 2048), BF16),
            pltpu.VMEM((896, 2048), F32),
            pltpu.VMEM((4, 4, 896, 128), BF16),
            pltpu.VMEM((2, 896, 128), BF16),
            pltpu.VMEM((2, 896, 128), BF16),
            pltpu.VMEM((4, 896, 128), BF16),
            pltpu.VMEM((4, 896, 128), BF16),
            pltpu.VMEM((8, 896, 128), BF16),
            pltpu.VMEM((4, 4, 896, 128), BF16),
            pltpu.VMEM((128, 896), F32),
            pltpu.VMEM((128, 896), F32),
            pltpu.VMEM((896, 128), F32),
            pltpu.VMEM((896, 128), F32),
            pltpu.VMEM((128, 896), F32),
            pltpu.VMEM((128, 896), F32),
            pltpu.VMEM((2, 8, 128), F32),
            pltpu.VMEM((4, 8, 128), F32),
            pltpu.VMEM((4, 8, 128), F32),
            dma((7,)),
            dma((6,)), dma((6,)),
            dma((4,)), dma((4,)),
            dma((n,)), dma((n,)),
            dma((n, 2)), dma((n, 2)),
            dma((n, 2)), dma((n, 2)),
            dma((n,)), dma((n,)),
            dma((n,)), dma((n,)),
            dma((n,)), dma((n, 4)),
            dma((n,)), dma((n,)),
            dma((6,)), dma((6,)),
            dma((6,)), dma((6,)),
        ],
        compiler_params=pltpu.CompilerParams(
            collective_id=0, has_side_effects=True, vmem_limit_bytes=50 * 2**20
        ),
        cost_estimate=pl.CostEstimate(flops=3_760_000_000, bytes_accessed=12_000_000, transcendentals=0),
    )(params[0], hidden_acts[0], out_grads[0], step_counts, outer_z.T, outer_x.T)
    return new_z.T, new_x.T, new_y


def solution(mesh):
    split = Mesh(mesh.devices.reshape(4, 4, 2, 2, 4), ("zl", "y", "c", "zh", "x"))
    rep, fsdp = ("zl", "y", "c"), ("zh", "x")
    placed = (
        P(rep, fsdp, None),
        P(rep, fsdp, None),
        P(rep, fsdp, None),
        P(rep),
        P(fsdp, rep),
        P(fsdp, rep),
    )
    return jax.shard_map(
        local,
        mesh=split,
        in_specs=placed,
        out_specs=(P(fsdp, rep), P(fsdp, rep), P(fsdp, None)),
        check_vma=False,
    )
```
